32 devices in a mesh: space: 8 (over z, x), tm: 4 (over y, core).
Axes of the slice: x: 2, y: 2, z: 4, core: 2. Of those that a mesh axis runs over, the one named last changes fastest.
Arguments:
- frame_slab: float32 [16384, 2048], P('space', 'tm'), may hold values from -160 to 160
- pair_decay_rates: float32 [32], replicated, may hold values from -2 to 0.5
- pair_angular_frequencies: float32 [32], replicated, as said below
Outputs:
- spatial_modes: float32 [64, 16384], P(None, 'space')
- misfit_matrix: float32 [16384, 2048], P('space', 'tm')
- gradient: float32 [64], replicated
- gauss_newton: float32 [64, 64], replicated
The draws below stay inside these ranges and needn't reach their ends.
Inputs may be any that keep to these rules, and one draw needn't show every extreme that they name: pair_angular_frequencies[k] lies within 0.5 of 2 pi (k + 1).
All inputs are finite; a program needn't handle non-finite values.
Results may differ from the reference program's by a relative error of at most 0.0003.
Values sent between devices are 32-bit elements; how exact they have to be, the bound alone decides.
A program may use at most 64 MiB of HBM per device.

```python
import jax
import jax.numpy as jnp
from jax import lax

PAIRS = 32
NP = 16384
FRAME_NUMBER = 2048
N_SPACE = 8


def draw_frame_slab(key, part):
    key = jax.random.fold_in(key, 11)
    streams = jax.random.split(key, 7)
    positions = jnp.arange(NP, dtype=jnp.float32) / NP
    measured_epochs = jnp.arange(FRAME_NUMBER, dtype=jnp.float32) / FRAME_NUMBER
    multiplier_power = jax.random.uniform(streams[0], (4,), minval=-1.5, maxval=0.3)
    cycle_spacings = jax.random.uniform(streams[1], (4,), minval=5.0, maxval=150.0)
    amplitudes = jax.random.uniform(streams[2], (NP, 4), minval=-1.0, maxval=1.0)
    argument_radians = jax.random.uniform(streams[3], (NP, 4), minval=-jnp.pi, maxval=jnp.pi)
    signal = jnp.zeros((NP, FRAME_NUMBER), jnp.float32)
    for mode_profile_entry in range(4):
        cycle_cosine_term = jnp.exp(multiplier_power[mode_profile_entry] * measured_epochs)[None, :] * jnp.cos(cycle_spacings[mode_profile_entry] * measured_epochs[None, :] + argument_radians[:, mode_profile_entry:mode_profile_entry + 1])
        signal = signal + amplitudes[:, mode_profile_entry:mode_profile_entry + 1] * cycle_cosine_term
    noise_part = jax.random.truncated_normal(streams[4], -4.0, 4.0, (NP, FRAME_NUMBER))
    spread = jnp.log(10.0)
    levels = jax.random.uniform(streams[5], (NP,), minval=0.0, maxval=1.0)
    row_scale = jnp.exp(jnp.log(3.0) * positions + levels * (spread - jnp.log(3.0)))
    noise_level = jnp.exp(jax.random.uniform(streams[6], (1, FRAME_NUMBER), minval=jnp.log(0.3), maxval=jnp.log(0.9)))
    return (row_scale[:, None] * (signal + noise_level * noise_part)).astype(jnp.float32)


def draw_pair_angular_frequencies(key, part):
    key = jax.random.fold_in(key, 5)
    offsets = jax.random.uniform(key, (PAIRS,), minval=-0.5, maxval=0.5)
    return (2.0 * jnp.pi * (jnp.arange(PAIRS, dtype=jnp.float32) + 1.0) + offsets).astype(jnp.float32)


def setup_inputs(seed: int = 0) -> dict:
    key_list = jax.random.split(jax.random.key(seed), 4)
    frame_slab = draw_frame_slab(jax.random.fold_in(key_list[3], 71), 0)
    pair_decay_rates = jnp.clip(jax.random.uniform(key_list[1], (PAIRS,), jnp.float32, -2.0, 0.5), -2.0, 0.5)
    pair_angular_frequencies = draw_pair_angular_frequencies(jax.random.fold_in(key_list[3], 71), 0)
    return dict(frame_slab=frame_slab, pair_decay_rates=pair_decay_rates, pair_angular_frequencies=pair_angular_frequencies)


highest = lax.Precision.HIGHEST

def build_epoch_vectors(pair_decay_rates, pair_angular_frequencies, measured_epochs):
    shrinking_exponential = jnp.exp(pair_decay_rates[:, None] * measured_epochs[None, :])
    turning_radians = pair_angular_frequencies[:, None] * measured_epochs[None, :]
    joined_vectors = jnp.stack([shrinking_exponential * jnp.cos(turning_radians), shrinking_exponential * jnp.sin(turning_radians)], axis=1)
    return joined_vectors.reshape(2 * pair_decay_rates.shape[0], measured_epochs.shape[0])

def coupling_table():
    return jnp.array([[[1.0, 0.0], [0.0, 1.0]], [[0.0, -1.0], [1.0, 0.0]]], dtype=jnp.float32)

def newton_terms(cross_term, mode_gram, slope_gram, magnitude_divisor):
    pairs = cross_term.shape[0] // 2
    coupling = coupling_table()
    cross_blocks = cross_term.reshape(pairs, 2, pairs, 2)
    indices = jnp.arange(pairs, dtype=jnp.int32)
    diagonal_blocks = cross_blocks[indices, :, indices, :]
    gradient = -magnitude_divisor * jnp.einsum('puw,kuw->kp', coupling, diagonal_blocks, precision=highest)
    mode_blocks = mode_gram.reshape(pairs, 2, pairs, 2)
    slope_blocks = slope_gram.reshape(pairs, 2, pairs, 2)
    inner = jnp.einsum('kulv,kwlx->kuwlvx', mode_blocks, slope_blocks, precision=highest)
    gauss_newton = magnitude_divisor * jnp.einsum('puw,kuwlvx,qvx->kplq', coupling, inner, coupling, precision=highest)
    return (gradient.reshape(2 * pairs), gauss_newton.reshape(2 * pairs, 2 * pairs))

def reference(frame_slab, pair_decay_rates, pair_angular_frequencies):
    location_number, complete_epochs = frame_slab.shape
    measured_epochs = jnp.arange(complete_epochs, dtype=jnp.float32) / complete_epochs
    epoch_vector_set = build_epoch_vectors(pair_decay_rates, pair_angular_frequencies, measured_epochs)
    jacobian_lines = epoch_vector_set * measured_epochs[None, :]
    basis_gram = jnp.dot(epoch_vector_set.astype(jnp.float32), epoch_vector_set.T.astype(jnp.float32), precision=highest, preferred_element_type=jnp.float32)
    slope_gram = jnp.dot(jacobian_lines.astype(jnp.float32), jacobian_lines.T.astype(jnp.float32), precision=highest, preferred_element_type=jnp.float32)
    projection = lax.dot_general(epoch_vector_set.astype(jnp.float32), frame_slab.astype(jnp.float32), (((1,), (1,)), ((), ())), precision=highest, preferred_element_type=jnp.float32)
    factor = jnp.linalg.cholesky(basis_gram)
    spatial_modes = jax.scipy.linalg.cho_solve((factor, True), projection)
    segment_locations = location_number // N_SPACE
    segment_list = frame_slab.reshape(N_SPACE, segment_locations, complete_epochs)
    mode_blocks = spatial_modes.reshape(-1, N_SPACE, segment_locations).transpose(1, 0, 2)

    def block_terms(block_pair):
        block_rows, block_modes = block_pair
        fitted = lax.dot_general(block_modes.astype(jnp.float32), epoch_vector_set.astype(jnp.float32), (((0,), (0,)), ((), ())), precision=highest, preferred_element_type=jnp.float32)
        block_residual = block_rows - fitted
        moment = lax.dot_general(block_residual.astype(jnp.float32), jacobian_lines.astype(jnp.float32), (((1,), (1,)), ((), ())), precision=highest, preferred_element_type=jnp.float32)
        return (block_residual, jnp.dot(block_modes.astype(jnp.float32), moment.astype(jnp.float32), precision=highest, preferred_element_type=jnp.float32))
    misfit_segments, cross_parts = lax.map(block_terms, (segment_list, mode_blocks))
    misfit_matrix = misfit_segments.reshape(location_number, complete_epochs)
    cross_term = jnp.sum(cross_parts, axis=0)
    mode_gram = jnp.dot(spatial_modes.astype(jnp.float32), spatial_modes.T.astype(jnp.float32), precision=highest, preferred_element_type=jnp.float32)
    magnitude_divisor = 1.0 / (location_number * complete_epochs)
    gradient, gauss_newton = newton_terms(cross_term, mode_gram, slope_gram, magnitude_divisor)
    return (spatial_modes, misfit_matrix, gradient, gauss_newton)
```

```python
import functools

import jax
import jax.numpy as jnp
from jax import lax
from jax.experimental import pallas as pl
from jax.experimental.pallas import tpu as pltpu
from jax.sharding import PartitionSpec as P

f32 = jnp.float32
bf16 = jnp.bfloat16
highest = lax.Precision.HIGHEST
NN = (((1,), (0,)), ((), ()))
NT = (((1,), (1,)), ((), ()))
TN = (((0,), (0,)), ((), ()))
MESH = pl.DeviceIdType.MESH
CHUNK = 256
HALF = CHUNK // 2
BLOCK = 128


def dot(a, b, dims, precision=None):
    return lax.dot_general(a, b, dims, precision=precision, preferred_element_type=f32)


def split(x):
    hi = x.astype(bf16)
    return hi, (x - hi.astype(f32)).astype(bf16)


def iota(shape, dim):
    return lax.broadcasted_iota(jnp.int32, shape, dim)


def kernel(
    n_space, n_tm, total_points,
    frame, rates, freqs,
    modes_out, misfit_out, grad_out, newton_out,
    slab, basis, slopes, part, modes, from_core, from_y, gram2, slope_gram, sums1, sums2,
    in_sem, out_sem, modes_sem, s1_send, s1_recv, y_send, y_recv, ag_send, ag_recv,
    p1_send, p1_recv, p2_send, p2_recv,
):
    points, epochs = slab.shape
    rows = 2 * rates.shape[1]
    chunks = points // CHUNK
    n_y = n_tm // 2
    total_epochs = epochs * n_tm
    share = rows // n_tm
    si, ti = lax.axis_index("space"), lax.axis_index("tm")
    yi, core = ti // 2, lax.rem(ti, 2)
    sibling = yi * 2 + (1 - core)

    def load(c):
        at = pl.ds(c * CHUNK, CHUNK)
        return pltpu.make_async_copy(frame.at[at], slab.at[at], in_sem.at[c])

    for c in range(chunks):
        load(c).start()

    space_peers = [lax.rem(si + d, n_space) for d in range(1, n_space)]
    tm_peers = [lax.rem(ti + d, n_tm) for d in range(1, n_tm)]
    barrier = pltpu.get_barrier_semaphore()
    for peer in space_peers:
        pl.semaphore_signal(barrier, inc=1, device_id={"space": peer}, device_id_type=MESH)
    for peer in tm_peers:
        pl.semaphore_signal(barrier, inc=1, device_id={"tm": peer}, device_id_type=MESH)

    pair_mask = iota((rows, rows // 2), 0) // 2 == iota((rows, rows // 2), 1)
    rate = jnp.sum(jnp.where(pair_mask, rates[...], 0.0), axis=1, keepdims=True)
    freq = jnp.sum(jnp.where(pair_mask, freqs[...], 0.0), axis=1, keepdims=True)
    lane = iota((rows, BLOCK), 1).astype(f32)
    even = lax.rem(iota((rows, BLOCK), 0), 2) == 0
    fine_t = lane / total_epochs
    coarse_t = lane * (BLOCK / total_epochs)
    fine_e = jnp.exp(rate * fine_t)
    fine_c = fine_e * jnp.cos(freq * fine_t)
    fine_s = fine_e * jnp.sin(freq * fine_t)
    coarse_e = jnp.exp(rate * jnp.minimum(coarse_t, 1.0))
    ca = coarse_e * jnp.cos(freq * coarse_t)
    sa = coarse_e * jnp.sin(freq * coarse_t)
    first = jnp.where(even, ca, sa)
    second = jnp.where(even, -sa, ca)
    for b in range(total_epochs // BLOCK):
        basis[:, b * BLOCK:(b + 1) * BLOCK] = (
            first[:, b:b + 1] * fine_c + second[:, b:b + 1] * fine_s
        )
    here = pl.ds(pl.multiple_of(ti * epochs, epochs), epochs)
    b_hi, b_lo = split(basis[:, here])
    b_two = jnp.concatenate([b_hi, b_lo], axis=0)
    pl.semaphore_wait(barrier, n_space + n_tm - 2)

    def half(c, who):
        return pl.ds(pl.multiple_of(c * CHUNK + who * HALF, HALF), HALF)

    def core_copy(c):
        return pltpu.make_async_remote_copy(
            part.at[:, half(c, 1 - core)], from_core.at[c], s1_send.at[c], s1_recv.at[c],
            device_id={"tm": sibling}, device_id_type=MESH)

    def y_copy(c, d, slot):
        peer = lax.rem(yi + d, n_y) * 2 + core
        return pltpu.make_async_remote_copy(
            from_y.at[c, slot], from_y.at[c, slot], y_send.at[c, d], y_recv.at[c, slot],
            device_id={"tm": peer}, device_id_type=MESH)

    def modes_copy(c, who):
        at = half(c, who)
        return pltpu.make_async_remote_copy(
            modes.at[:, at], modes.at[:, at], ag_send.at[c], ag_recv.at[c],
            device_id={"tm": sibling}, device_id_type=MESH)

    def pass_on(c):
        core_copy(c).wait_recv()
        from_y[c, yi] = part[:, half(c, core)] + from_core[c]
        for d in range(1, n_y):
            y_copy(c, d, yi).start()

    for c in range(chunks):
        load(c).wait()
        f_hi, f_lo = split(slab[c * CHUNK:(c + 1) * CHUNK, :])
        two = dot(b_two, f_hi, NT)
        part[:, c * CHUNK:(c + 1) * CHUNK] = (two[rows:] + dot(b_hi, f_lo, NT)) + two[:rows]
        core_copy(c).start()
        if c:
            pass_on(c - 1)
    pass_on(chunks - 1)

    gram = dot(basis[...], basis[...], NT, highest)
    eye = (iota((rows, rows), 0) == iota((rows, rows), 1)).astype(f32)
    aug = jnp.concatenate([gram, eye], axis=1)
    row_id = iota(aug.shape, 0)
    for k in range(rows):
        pivot = aug[k:k + 1, :] / aug[k:k + 1, k:k + 1]
        aug = jnp.where(row_id == k, pivot, aug - aug[:, k:k + 1] * pivot)
    inverse = aug[:, rows:]

    first2 = jnp.where(even, -sa, ca)
    second2 = jnp.where(even, -ca, -sa)
    for b in range(total_epochs // BLOCK):
        at = slice(b * BLOCK, (b + 1) * BLOCK)
        t = fine_t + b * (BLOCK / total_epochs)
        slopes[:rows, at] = basis[:, at] * t
        slopes[rows:, at] = (first2[:, b:b + 1] * fine_c + second2[:, b:b + 1] * fine_s) * t
    j_hi, j_lo = split(slopes[...])
    cross = dot(j_lo, j_hi, NT)
    slope_gram[...] = dot(j_hi, j_hi, NT) + (cross + cross.T)

    b_three = jnp.concatenate([b_hi, b_hi, b_lo], axis=0)
    moment = jnp.zeros((rows, epochs), f32)
    gram_two = jnp.zeros((2 * rows, rows), f32)

    def solve(c):
        for d in range(1, n_y):
            y_copy(c, d, lax.rem(yi + d, n_y)).wait_recv()
        total = from_y[c, 0]
        for y in range(1, n_y):
            total = total + from_y[c, y]
        modes[:, half(c, core)] = dot(inverse, total, NN, highest)
        modes_copy(c, core).start()

    def store(c):
        at = pl.ds(c * CHUNK, CHUNK)
        return (pltpu.make_async_copy(slab.at[at], misfit_out.at[at], out_sem.at[c]),
                pltpu.make_async_copy(modes.at[:, at], modes_out.at[:, at], modes_sem.at[c]))

    solve(0)
    for c in range(chunks):
        if c + 1 < chunks:
            solve(c + 1)
        modes_copy(c, 1 - core).wait_recv()
        at = slice(c * CHUNK, (c + 1) * CHUNK)
        s_hi, s_lo = split(modes[:, at])
        fitted = dot(jnp.concatenate([s_hi, s_lo, s_hi], axis=0), b_three, TN)
        misfit = slab[at, :] - fitted
        slab[at, :] = misfit
        for copy in store(c):
            copy.start()
        m_hi, m_lo = split(misfit)
        s_two = jnp.concatenate([s_hi, s_lo], axis=0)
        two = dot(s_two, m_hi, NN)
        moment = moment + ((two[rows:] + dot(s_hi, m_lo, NN)) + two[:rows])
        gram_two = gram_two + dot(s_two, s_hi, NT)

    low = gram_two[rows:]
    mode_gram = gram_two[:rows] + (low + low.T)
    gram2[...] = jnp.concatenate([mode_gram, mode_gram], axis=1)
    decay = jnp.sum(moment * slopes[:rows, here], axis=1, keepdims=True)
    turn = jnp.sum(moment * slopes[rows:, here], axis=1, keepdims=True)
    r64, c64 = iota((rows, rows), 0), iota((rows, rows), 1)
    picked = jnp.where(lax.rem(c64, 2) == 0, decay, turn)
    grad = jnp.sum(jnp.where(r64 // 2 == c64 // 2, picked, 0.0), axis=0, keepdims=True)
    zeros = jnp.zeros((7, 2 * rows), f32)
    wide = jnp.concatenate([grad, jnp.zeros_like(grad)], axis=1)
    mine = pl.ds(pl.multiple_of(ti * share, share), share)
    sums1[si, :share, :] = gram2[mine, :]
    sums1[si, share:, :] = jnp.concatenate([wide, zeros], axis=0)

    def copy1(d, slot):
        return pltpu.make_async_remote_copy(
            sums1.at[slot], sums1.at[slot], p1_send.at[d], p1_recv.at[slot],
            device_id={"space": lax.rem(si + d, n_space)}, device_id_type=MESH)

    def copy2(d, slot):
        return pltpu.make_async_remote_copy(
            sums2.at[slot], sums2.at[slot], p2_send.at[d], p2_recv.at[slot],
            device_id={"tm": lax.rem(ti + d, n_tm)}, device_id_type=MESH)

    for d in range(1, n_space):
        copy1(d, si).start()
    for d in range(1, n_space):
        copy1(d, lax.rem(si + d, n_space)).wait_recv()
    total = sums1[0]
    for s in range(1, n_space):
        total = total + sums1[s]
    scale = 1.0 / (total_points * total_epochs)
    below = pl.ds(pl.multiple_of(ti * share + rows, share), share)
    m2 = total[:share]
    both = jnp.concatenate([m2 * slope_gram[mine, :], m2 * slope_gram[below, :]], axis=0)
    u, v = iota((2 * rows, rows), 0), iota((2 * rows, rows), 1)
    take_cols = jnp.where((lax.rem(u, rows) // 2 == v // 2) & (u // rows == lax.rem(v, 2)), 1.0, 0.0)
    u, v = iota((share, 2 * share), 0), iota((share, 2 * share), 1)
    take_rows = jnp.where((lax.rem(v, share) // 2 == u // 2) & (v // share == lax.rem(u, 2)), 1.0, 0.0)
    newton = scale * dot(take_rows, dot(both, take_cols, NN, highest), NN, highest)
    sums2[ti, :share, :] = jnp.concatenate([newton, jnp.zeros_like(newton)], axis=1)
    sums2[ti, share:, :] = total[share:] * -scale
    for d in range(1, n_tm):
        copy2(d, ti).start()
    for d in range(1, n_tm):
        copy2(d, lax.rem(ti + d, n_tm)).wait_recv()
    gradient = sums2[0, share:share + 1, :rows]
    for j in range(n_tm):
        newton_out[j * share:(j + 1) * share, :] = sums2[j, :share, :rows]
        if j:
            gradient = gradient + sums2[j, share:share + 1, :rows]
    grad_out[...] = gradient

    for c in range(chunks):
        core_copy(c).wait_send()
        for d in range(1, n_y):
            y_copy(c, d, yi).wait_send()
        modes_copy(c, core).wait_send()
        for copy in store(c):
            copy.wait()
    for d in range(1, n_space):
        copy1(d, si).wait_send()
    for d in range(1, n_tm):
        copy2(d, ti).wait_send()


def local(n_space, n_tm, frame_slab, pair_decay_rates, pair_angular_frequencies):
    points, epochs = frame_slab.shape
    pairs = pair_decay_rates.shape[0]
    rows = 2 * pairs
    chunks = points // CHUNK
    n_y = n_tm // 2
    share = rows // n_tm
    any_space = pl.BlockSpec(memory_space=pl.ANY)
    vmem = pl.BlockSpec(memory_space=pltpu.VMEM)
    dma = pltpu.SemaphoreType.DMA
    modes, misfit, grad, newton = pl.pallas_call(
        functools.partial(kernel, n_space, n_tm, points * n_space),
        out_shape=(
            jax.ShapeDtypeStruct((rows, points), f32),
            jax.ShapeDtypeStruct((points, epochs), f32),
            jax.ShapeDtypeStruct((1, rows), f32),
            jax.ShapeDtypeStruct((rows, rows), f32),
        ),
        in_specs=[any_space, vmem, vmem],
        out_specs=(any_space, any_space, vmem, vmem),
        scratch_shapes=[
            pltpu.VMEM((points, epochs), f32),
            pltpu.VMEM((rows, epochs * n_tm), f32),
            pltpu.VMEM((2 * rows, epochs * n_tm), f32),
            pltpu.VMEM((rows, points), f32),
            pltpu.VMEM((rows, points), f32),
            pltpu.VMEM((chunks, rows, HALF), f32),
            pltpu.VMEM((chunks, n_y, rows, HALF), f32),
            pltpu.VMEM((rows, 2 * rows), f32),
            pltpu.VMEM((2 * rows, 2 * rows), f32),
            pltpu.VMEM((n_space, share + 8, 2 * rows), f32),
            pltpu.VMEM((n_tm, share + 8, 2 * rows), f32),
            dma((chunks,)), dma((chunks,)), dma((chunks,)),
            dma((chunks,)), dma((chunks,)),
            dma((chunks, n_y)), dma((chunks, n_y)),
            dma((chunks,)), dma((chunks,)),
            dma((n_space,)), dma((n_space,)),
            dma((n_tm,)), dma((n_tm,)),
        ],
        compiler_params=pltpu.CompilerParams(
            collective_id=0, has_side_effects=True, vmem_limit_bytes=48 * 2**20
        ),
    )(frame_slab, pair_decay_rates[None, :], pair_angular_frequencies[None, :])
    return modes, misfit, grad.reshape(rows), newton


def solution(mesh):
    return jax.shard_map(
        functools.partial(local, mesh.shape["space"], mesh.shape["tm"]),
        mesh=mesh,
        in_specs=(P("space", "tm"), P(), P()),
        out_specs=(P(None, "space"), P("space", "tm"), P(), P()),
        check_vma=False,
    )
```

```python
import functools

import jax
import jax.numpy as jnp
from jax import lax
from jax.experimental import pallas as pl
from jax.experimental.pallas import tpu as pltpu
from jax.sharding import PartitionSpec as P

f32 = jnp.float32
bf16 = jnp.bfloat16
highest = lax.Precision.HIGHEST
NN = (((1,), (0,)), ((), ()))
NT = (((1,), (1,)), ((), ()))
TN = (((0,), (0,)), ((), ()))
MESH = pl.DeviceIdType.MESH
CHUNK = 256
HALF = CHUNK // 2
AHEAD = 2
BLOCK = 128


def dot(a, b, dims, precision=None):
    return lax.dot_general(a, b, dims, precision=precision, preferred_element_type=f32)


def split(x):
    hi = x.astype(bf16)
    return hi, (x - hi.astype(f32)).astype(bf16)


def iota(shape, dim):
    return lax.broadcasted_iota(jnp.int32, shape, dim)


def kernel(
    n_space, n_tm, total_points,
    frame, rates_in, freqs_in,
    modes, slab, grad_out, newton_out,
    rates, freqs, basis, slopes, part, from_core, from_y, gram2, slope_gram, sums1, sums2,
    in_sem, par_sem, s1_send, s1_recv, y_send, y_recv, ag_send, ag_recv,
    p1_send, p1_recv, p2_send, p2_recv,
):
    points, epochs = slab.shape
    rows = 2 * rates.shape[1]
    chunks = points // CHUNK
    n_y = n_tm // 2
    total_epochs = epochs * n_tm
    share = rows // n_tm
    si, ti = lax.axis_index("space"), lax.axis_index("tm")
    yi, core = ti // 2, lax.rem(ti, 2)
    sibling = yi * 2 + (1 - core)

    def load(c):
        at = pl.ds(c * CHUNK, CHUNK)
        return pltpu.make_async_copy(frame.at[at], slab.at[at], in_sem.at[c])

    parameters = [pltpu.make_async_copy(rates_in, rates, par_sem.at[0]),
                  pltpu.make_async_copy(freqs_in, freqs, par_sem.at[1])]
    for copy in parameters:
        copy.start()
    for c in range(chunks):
        load(c).start()

    space_peers = [lax.rem(si + d, n_space) for d in range(1, n_space)]
    tm_peers = [lax.rem(ti + d, n_tm) for d in range(1, n_tm)]
    barrier = pltpu.get_barrier_semaphore()
    for peer in space_peers:
        pl.semaphore_signal(barrier, inc=1, device_id={"space": peer}, device_id_type=MESH)
    for peer in tm_peers:
        pl.semaphore_signal(barrier, inc=1, device_id={"tm": peer}, device_id_type=MESH)

    for copy in parameters:
        copy.wait()
    pair_mask = iota((rows, rows // 2), 0) // 2 == iota((rows, rows // 2), 1)
    rate = jnp.sum(jnp.where(pair_mask, rates[...], 0.0), axis=1, keepdims=True)
    freq = jnp.sum(jnp.where(pair_mask, freqs[...], 0.0), axis=1, keepdims=True)
    lane = iota((rows, BLOCK), 1).astype(f32)
    even = lax.rem(iota((rows, BLOCK), 0), 2) == 0
    fine_t = lane / total_epochs
    coarse_t = lane * (BLOCK / total_epochs)
    fine_e = jnp.exp(rate * fine_t)
    fine_c = fine_e * jnp.cos(freq * fine_t)
    fine_s = fine_e * jnp.sin(freq * fine_t)
    coarse_e = jnp.exp(rate * jnp.minimum(coarse_t, 1.0))
    ca = coarse_e * jnp.cos(freq * coarse_t)
    sa = coarse_e * jnp.sin(freq * coarse_t)
    first = jnp.where(even, ca, sa)
    second = jnp.where(even, -sa, ca)
    for b in range(total_epochs // BLOCK):
        basis[:, b * BLOCK:(b + 1) * BLOCK] = (
            first[:, b:b + 1] * fine_c + second[:, b:b + 1] * fine_s
        )
    here = pl.ds(pl.multiple_of(ti * epochs, epochs), epochs)
    b_hi, b_lo = split(basis[:, here])
    b_two = jnp.concatenate([b_hi, b_lo], axis=0)

    gram = dot(basis[...], basis[...], NT, highest)
    eye = (iota((rows, rows), 0) == iota((rows, rows), 1)).astype(f32)
    augmented = jnp.concatenate([gram, eye], axis=1)
    tiles = [augmented[i:i + 8] for i in range(0, rows, 8)]
    row_id = iota((8, 2 * rows), 0)

    def eliminate(k):
        own, o = k // 8, k % 8
        r0, r1 = tiles[own][o:o + 1], tiles[own][o + 1:o + 2]
        a, b = r0[:, k:k + 1], r0[:, k + 1:k + 2]
        c, d = r1[:, k:k + 1], r1[:, k + 1:k + 2]
        scale = 1.0 / (a * d - b * c)
        p0 = (d * r0 - b * r1) * scale
        p1 = (a * r1 - c * r0) * scale
        for i in range(len(tiles)):
            t = tiles[i]
            tiles[i] = t - t[:, k:k + 1] * p0 - t[:, k + 1:k + 2] * p1
        tiles[own] = jnp.where(row_id == o, p0, jnp.where(row_id == o + 1, p1, tiles[own]))

    pl.semaphore_wait(barrier, n_space + n_tm - 2)

    def half(c, who):
        return pl.ds(pl.multiple_of(c * CHUNK + who * HALF, HALF), HALF)

    def core_copy(c):
        return pltpu.make_async_remote_copy(
            part.at[:, half(c, 1 - core)], from_core.at[c], s1_send.at[c], s1_recv.at[c],
            device_id={"tm": sibling}, device_id_type=MESH)

    def y_copy(c, d, slot):
        peer = lax.rem(yi + d, n_y) * 2 + core
        return pltpu.make_async_remote_copy(
            from_y.at[c, slot], from_y.at[c, slot], y_send.at[c, d], y_recv.at[c, slot],
            device_id={"tm": peer}, device_id_type=MESH)

    def modes_copy(c, who):
        at = half(c, who)
        return pltpu.make_async_remote_copy(
            modes.at[:, at], modes.at[:, at], ag_send.at[c], ag_recv.at[c],
            device_id={"tm": sibling}, device_id_type=MESH)

    def pass_on(c):
        core_copy(c).wait_recv()
        from_y[c, yi] = part[:, half(c, core)] + from_core[c]
        for d in range(1, n_y):
            y_copy(c, d, yi).start()

    for c in range(chunks):
        load(c).wait()
        f_hi, f_lo = split(slab[c * CHUNK:(c + 1) * CHUNK, :])
        two = dot(b_two, f_hi, NT)
        part[:, c * CHUNK:(c + 1) * CHUNK] = (two[rows:] + dot(b_hi, f_lo, NT)) + two[:rows]
        for k in range(rows * c // chunks, rows * (c + 1) // chunks, 2):
            eliminate(k)
        core_copy(c).start()
        if c:
            pass_on(c - 1)
    pass_on(chunks - 1)

    inverse = jnp.concatenate(tiles, axis=0)[:, rows:]

    first2 = jnp.where(even, -sa, ca)
    second2 = jnp.where(even, -ca, -sa)
    for b in range(total_epochs // BLOCK):
        at = slice(b * BLOCK, (b + 1) * BLOCK)
        t = fine_t + b * (BLOCK / total_epochs)
        slopes[:rows, at] = basis[:, at] * t
        slopes[rows:, at] = (first2[:, b:b + 1] * fine_c + second2[:, b:b + 1] * fine_s) * t
    j_hi, j_lo = split(slopes[...])
    cross = dot(j_lo, j_hi, NT)
    slope_gram[...] = dot(j_hi, j_hi, NT) + (cross + cross.T)

    b_three = jnp.concatenate([b_hi, b_hi, b_lo], axis=0)
    moment = jnp.zeros((rows, epochs), f32)
    gram_two = jnp.zeros((2 * rows, rows), f32)

    def solve(c):
        for d in range(1, n_y):
            y_copy(c, d, lax.rem(yi + d, n_y)).wait_recv()
        total = from_y[c, 0]
        for y in range(1, n_y):
            total = total + from_y[c, y]
        modes[:, half(c, core)] = dot(inverse, total, NN, highest)
        modes_copy(c, core).start()

    for c in range(min(AHEAD, chunks)):
        solve(c)
    for c in range(chunks):
        if c + AHEAD < chunks:
            solve(c + AHEAD)
        modes_copy(c, 1 - core).wait_recv()
        at = slice(c * CHUNK, (c + 1) * CHUNK)
        s_hi, s_lo = split(modes[:, at])
        fitted = dot(jnp.concatenate([s_hi, s_lo, s_hi], axis=0), b_three, TN)
        misfit = slab[at, :] - fitted
        slab[at, :] = misfit
        m_hi, m_lo = split(misfit)
        s_two = jnp.concatenate([s_hi, s_lo], axis=0)
        two = dot(s_two, m_hi, NN)
        moment = moment + ((two[rows:] + dot(s_hi, m_lo, NN)) + two[:rows])
        gram_two = gram_two + dot(s_two, s_hi, NT)

    low = gram_two[rows:]
    mode_gram = gram_two[:rows] + (low + low.T)
    gram2[...] = jnp.concatenate([mode_gram, mode_gram], axis=1)
    decay = jnp.sum(moment * slopes[:rows, here], axis=1, keepdims=True)
    turn = jnp.sum(moment * slopes[rows:, here], axis=1, keepdims=True)
    r64, c64 = iota((rows, rows), 0), iota((rows, rows), 1)
    picked = jnp.where(lax.rem(c64, 2) == 0, decay, turn)
    grad = jnp.sum(jnp.where(r64 // 2 == c64 // 2, picked, 0.0), axis=0, keepdims=True)
    zeros = jnp.zeros((7, 2 * rows), f32)
    wide = jnp.concatenate([grad, jnp.zeros_like(grad)], axis=1)
    mine = pl.ds(pl.multiple_of(ti * share, share), share)
    sums1[si, :share, :] = gram2[mine, :]
    sums1[si, share:, :] = jnp.concatenate([wide, zeros], axis=0)

    def copy1(d, slot):
        return pltpu.make_async_remote_copy(
            sums1.at[slot], sums1.at[slot], p1_send.at[d], p1_recv.at[slot],
            device_id={"space": lax.rem(si + d, n_space)}, device_id_type=MESH)

    def copy2(d, slot):
        return pltpu.make_async_remote_copy(
            sums2.at[slot], sums2.at[slot], p2_send.at[d], p2_recv.at[slot],
            device_id={"tm": lax.rem(ti + d, n_tm)}, device_id_type=MESH)

    for d in range(1, n_space):
        copy1(d, si).start()
    for d in range(1, n_space):
        copy1(d, lax.rem(si + d, n_space)).wait_recv()
    total = sums1[0]
    for s in range(1, n_space):
        total = total + sums1[s]
    scale = 1.0 / (total_points * total_epochs)
    below = pl.ds(pl.multiple_of(ti * share + rows, share), share)
    m2 = total[:share]
    both = jnp.concatenate([m2 * slope_gram[mine, :], m2 * slope_gram[below, :]], axis=0)
    u, v = iota((2 * rows, rows), 0), iota((2 * rows, rows), 1)
    take_cols = jnp.where((lax.rem(u, rows) // 2 == v // 2) & (u // rows == lax.rem(v, 2)), 1.0, 0.0)
    u, v = iota((share, 2 * share), 0), iota((share, 2 * share), 1)
    take_rows = jnp.where((lax.rem(v, share) // 2 == u // 2) & (v // share == lax.rem(u, 2)), 1.0, 0.0)
    newton = scale * dot(take_rows, dot(both, take_cols, NN, highest), NN, highest)
    sums2[ti, :share, :] = jnp.concatenate([newton, jnp.zeros_like(newton)], axis=1)
    sums2[ti, share:, :] = total[share:] * -scale
    for d in range(1, n_tm):
        copy2(d, ti).start()
    for d in range(1, n_tm):
        copy2(d, lax.rem(ti + d, n_tm)).wait_recv()
    gradient = sums2[0, share:share + 1, :rows]
    for j in range(n_tm):
        newton_out[j * share:(j + 1) * share, :] = sums2[j, :share, :rows]
        if j:
            gradient = gradient + sums2[j, share:share + 1, :rows]
    grad_out[...] = gradient

    for c in range(chunks):
        core_copy(c).wait_send()
        for d in range(1, n_y):
            y_copy(c, d, yi).wait_send()
        modes_copy(c, core).wait_send()
    for d in range(1, n_space):
        copy1(d, si).wait_send()
    for d in range(1, n_tm):
        copy2(d, ti).wait_send()


def write_out(modes, misfit, grad, newton, modes_out, misfit_out, grad_out, newton_out, sem):
    points = misfit.shape[0]
    pieces = [pl.ds(i * (points // 8), points // 8) for i in range(8)]
    copies = [(misfit.at[p], misfit_out.at[p]) for p in pieces]
    copies += [(modes, modes_out), (newton, newton_out), (grad, grad_out)]
    copies = [pltpu.make_async_copy(a, b, sem.at[i]) for i, (a, b) in enumerate(copies)]
    for copy in copies:
        copy.start()
    for copy in copies:
        copy.wait()


def local(n_space, n_tm, frame_slab, pair_decay_rates, pair_angular_frequencies):
    points, epochs = frame_slab.shape
    pairs = pair_decay_rates.shape[0]
    rows = 2 * pairs
    chunks = points // CHUNK
    n_y = n_tm // 2
    share = rows // n_tm
    hbm = pl.BlockSpec(memory_space=pltpu.HBM)
    any_space = pl.BlockSpec(memory_space=pl.ANY)
    vmem = pl.BlockSpec(memory_space=pltpu.VMEM)
    dma = pltpu.SemaphoreType.DMA
    shapes = (
        jax.ShapeDtypeStruct((rows, points), f32),
        jax.ShapeDtypeStruct((points, epochs), f32),
        jax.ShapeDtypeStruct((1, rows), f32),
        jax.ShapeDtypeStruct((rows, rows), f32),
    )
    operands = (frame_slab, pair_decay_rates[None, :], pair_angular_frequencies[None, :])
    results = pl.pallas_call(
        functools.partial(kernel, n_space, n_tm, points * n_space),
        out_shape=shapes,
        in_specs=[hbm] * 3,
        out_specs=(vmem,) * 4,
        scratch_shapes=[
            pltpu.VMEM((1, pairs), f32),
            pltpu.VMEM((1, pairs), f32),
            pltpu.VMEM((rows, epochs * n_tm), f32),
            pltpu.VMEM((2 * rows, epochs * n_tm), f32),
            pltpu.VMEM((rows, points), f32),
            pltpu.VMEM((chunks, rows, HALF), f32),
            pltpu.VMEM((chunks, n_y, rows, HALF), f32),
            pltpu.VMEM((rows, 2 * rows), f32),
            pltpu.VMEM((2 * rows, 2 * rows), f32),
            pltpu.VMEM((n_space, share + 8, 2 * rows), f32),
            pltpu.VMEM((n_tm, share + 8, 2 * rows), f32),
            dma((chunks,)), dma((2,)),
            dma((chunks,)), dma((chunks,)),
            dma((chunks, n_y)), dma((chunks, n_y)),
            dma((chunks,)), dma((chunks,)),
            dma((n_space,)), dma((n_space,)),
            dma((n_tm,)), dma((n_tm,)),
        ],
        compiler_params=pltpu.CompilerParams(
            collective_id=0, has_side_effects=True, vmem_limit_bytes=48 * 2**20
        ),
    )(*(pltpu.with_memory_space_constraint(x, pltpu.HBM) for x in operands))
    modes, misfit, grad, newton = pl.pallas_call(
        write_out,
        out_shape=shapes,
        in_specs=[any_space] * 4,
        out_specs=(hbm,) * 4,
        scratch_shapes=[dma((12,))],
    )(*results)
    return modes, misfit, grad.reshape(rows), newton


def solution(mesh):
    return jax.shard_map(
        functools.partial(local, mesh.shape["space"], mesh.shape["tm"]),
        mesh=mesh,
        in_specs=(P("space", "tm"), P(), P()),
        out_specs=(P(None, "space"), P("space", "tm"), P(), P()),
        check_vma=False,
    )
```

```python
import functools

import jax
import jax.numpy as jnp
from jax import lax
from jax.experimental import pallas as pl
from jax.experimental.pallas import tpu as pltpu
from jax.sharding import PartitionSpec as P

f32 = jnp.float32
bf16 = jnp.bfloat16
highest = lax.Precision.HIGHEST
NN = (((1,), (0,)), ((), ()))
NT = (((1,), (1,)), ((), ()))
TN = (((0,), (0,)), ((), ()))
MESH = pl.DeviceIdType.MESH
CHUNK = 256
HALF = CHUNK // 2
AHEAD = 6
BLOCK = 128


def dot(a, b, dims, precision=None):
    return lax.dot_general(a, b, dims, precision=precision, preferred_element_type=f32)


def split(x):
    hi = x.astype(bf16)
    return hi, (x - hi.astype(f32)).astype(bf16)


def iota(shape, dim):
    return lax.broadcasted_iota(jnp.int32, shape, dim)


def cos_sin(x):
    n = jnp.floor(x * 0.6366197723675814 + 0.5)
    r = ((x - n * 1.5703125) - n * 0.0004837512969970703) - n * 7.549789948768648e-08
    z = r * r
    s = r + r * z * (-1.6666654611e-1 + z * (8.3321608736e-3 - z * 1.9515295891e-4))
    c = 1.0 - 0.5 * z + z * z * (
        4.166664568298827e-2 + z * (-1.388731625493765e-3 + z * 2.443315711809948e-5))
    q = n.astype(jnp.int32) & 3
    odd = (q & 1) == 1
    cos, sin = jnp.where(odd, s, c), jnp.where(odd, c, s)
    return (jnp.where((q == 1) | (q == 2), -cos, cos), jnp.where(q >= 2, -sin, sin))


def kernel(
    n_space, n_tm, total_points,
    frame, rates_in, freqs_in,
    modes, slab, grad_out, newton_out,
    rates, freqs, basis, slopes, part, from_core, from_y, gram2, slope_gram, sums1, sums2, grads,
    in_sem, par_sem, s1_send, s1_recv, y_send, y_recv, ag_send, ag_recv,
    p1_send, p1_recv, p2_send, p2_recv, g_send, g_recv,
):
    points, epochs = slab.shape
    rows = 2 * rates.shape[1]
    chunks = points // CHUNK
    n_y = n_tm // 2
    total_epochs = epochs * n_tm
    share = rows // n_tm
    si, ti = lax.axis_index("space"), lax.axis_index("tm")
    yi, core = ti // 2, lax.rem(ti, 2)
    sibling = yi * 2 + (1 - core)

    def load(c):
        at = pl.ds(c * CHUNK, CHUNK)
        return pltpu.make_async_copy(frame.at[at], slab.at[at], in_sem.at[c])

    parameters = [pltpu.make_async_copy(rates_in, rates, par_sem.at[0]),
                  pltpu.make_async_copy(freqs_in, freqs, par_sem.at[1])]
    for copy in parameters:
        copy.start()
    for c in range(chunks):
        load(c).start()

    devices = n_space * n_tm
    me = si * n_tm + ti

    def other(d):
        peer = lax.rem(me + d, devices)
        return (peer // n_tm, lax.rem(peer, n_tm))

    barrier = pltpu.get_barrier_semaphore()

    def greet(d, carry):
        pl.semaphore_signal(barrier, inc=1, device_id=other(d), device_id_type=MESH)
        return carry

    lax.fori_loop(1, devices, greet, 0)

    for copy in parameters:
        copy.wait()
    pair_mask = iota((rows, rows // 2), 0) // 2 == iota((rows, rows // 2), 1)
    rate = jnp.sum(jnp.where(pair_mask, rates[...], 0.0), axis=1, keepdims=True)
    freq = jnp.sum(jnp.where(pair_mask, freqs[...], 0.0), axis=1, keepdims=True)
    lane = iota((rows, BLOCK), 1).astype(f32)
    even = lax.rem(iota((rows, BLOCK), 0), 2) == 0
    fine_t = lane / total_epochs
    coarse_t = lane * (BLOCK / total_epochs)
    fine_e = jnp.exp(rate * fine_t)
    fine_c, fine_s = cos_sin(freq * fine_t)
    fine_c, fine_s = fine_e * fine_c, fine_e * fine_s
    coarse_t = jnp.minimum(coarse_t, 1.0)
    coarse_e = jnp.exp(rate * coarse_t)
    ca, sa = cos_sin(freq * coarse_t)
    ca, sa = coarse_e * ca, coarse_e * sa
    first = jnp.where(even, ca, sa)
    second = jnp.where(even, -sa, ca)
    for b in range(total_epochs // BLOCK):
        basis[:, b * BLOCK:(b + 1) * BLOCK] = (
            first[:, b:b + 1] * fine_c + second[:, b:b + 1] * fine_s
        )
    here = pl.ds(pl.multiple_of(ti * epochs, epochs), epochs)
    b_hi, b_lo = split(basis[:, here])
    b_two = jnp.concatenate([b_hi, b_lo], axis=0)

    gram = dot(basis[...], basis[...], NT, highest)
    eye = (iota((rows, rows), 0) == iota((rows, rows), 1)).astype(f32)
    augmented = jnp.concatenate([gram, eye], axis=1)
    tiles = [augmented[i:i + 8] for i in range(0, rows, 8)]
    row_id = iota((8, 2 * rows), 0)

    def eliminate(k):
        own, o = k // 8, k % 8
        r0, r1 = tiles[own][o:o + 1], tiles[own][o + 1:o + 2]
        a, b = r0[:, k:k + 1], r0[:, k + 1:k + 2]
        c, d = r1[:, k:k + 1], r1[:, k + 1:k + 2]
        scale = 1.0 / (a * d - b * c)
        p0 = (d * r0 - b * r1) * scale
        p1 = (a * r1 - c * r0) * scale
        for i in range(len(tiles)):
            t = tiles[i]
            tiles[i] = t - t[:, k:k + 1] * p0 - t[:, k + 1:k + 2] * p1
        tiles[own] = jnp.where(row_id == o, p0, jnp.where(row_id == o + 1, p1, tiles[own]))

    pl.semaphore_wait(barrier, devices - 1)

    def half(c, who):
        return pl.ds(pl.multiple_of(c * CHUNK + who * HALF, HALF), HALF)

    def core_copy(c):
        return pltpu.make_async_remote_copy(
            part.at[:, half(c, 1 - core)], from_core.at[c], s1_send.at[c], s1_recv.at[c],
            device_id={"tm": sibling}, device_id_type=MESH)

    def y_copy(c, d, slot):
        peer = lax.rem(yi + d, n_y) * 2 + core
        return pltpu.make_async_remote_copy(
            from_y.at[c, slot], from_y.at[c, slot], y_send.at[c, d], y_recv.at[c, slot],
            device_id={"tm": peer}, device_id_type=MESH)

    def modes_copy(c, who):
        at = half(c, who)
        return pltpu.make_async_remote_copy(
            modes.at[:, at], modes.at[:, at], ag_send.at[c], ag_recv.at[c],
            device_id={"tm": sibling}, device_id_type=MESH)

    def pass_on(c):
        core_copy(c).wait_recv()
        from_y[c, yi] = part[:, half(c, core)] + from_core[c]
        for d in range(1, n_y):
            y_copy(c, d, yi).start()

    for c in range(chunks):
        load(c).wait()
        f_hi, f_lo = split(slab[c * CHUNK:(c + 1) * CHUNK, :])
        two = dot(b_two, f_hi, NT)
        part[:, c * CHUNK:(c + 1) * CHUNK] = (two[rows:] + dot(b_hi, f_lo, NT)) + two[:rows]
        for k in range(rows * c // chunks, rows * (c + 1) // chunks, 2):
            eliminate(k)
        core_copy(c).start()
        if c:
            pass_on(c - 1)
    pass_on(chunks - 1)

    inverse = jnp.concatenate(tiles, axis=0)[:, rows:]

    first2 = jnp.where(even, -sa, ca)
    second2 = jnp.where(even, -ca, -sa)
    for b in range(total_epochs // BLOCK):
        at = slice(b * BLOCK, (b + 1) * BLOCK)
        t = fine_t + b * (BLOCK / total_epochs)
        slopes[:rows, at] = basis[:, at] * t
        slopes[rows:, at] = (first2[:, b:b + 1] * fine_c + second2[:, b:b + 1] * fine_s) * t
    j_hi, j_lo = split(slopes[...])
    cross = dot(j_lo, j_hi, NT)
    slope_gram[...] = dot(j_hi, j_hi, NT) + (cross + cross.T)

    b_three = jnp.concatenate([b_hi, b_hi, b_lo], axis=0)
    moment = jnp.zeros((rows, epochs), f32)

    def solve(c):
        for d in range(1, n_y):
            y_copy(c, d, lax.rem(yi + d, n_y)).wait_recv()
        total = from_y[c, 0]
        for y in range(1, n_y):
            total = total + from_y[c, y]
        modes[:, half(c, core)] = dot(inverse, total, NN, highest)
        modes_copy(c, core).start()

    mine = pl.ds(pl.multiple_of(ti * share, share), share)
    below = pl.ds(pl.multiple_of(ti * share + rows, share), share)
    scale = 1.0 / (total_points * total_epochs)

    def copy1(d, slot):
        return pltpu.make_async_remote_copy(
            sums1.at[slot], sums1.at[slot], p1_send.at[d], p1_recv.at[slot],
            device_id={"space": lax.rem(si + d, n_space)}, device_id_type=MESH)

    def copy2(d, slot):
        return pltpu.make_async_remote_copy(
            sums2.at[slot], sums2.at[slot], p2_send.at[d], p2_recv.at[slot],
            device_id={"tm": lax.rem(ti + d, n_tm)}, device_id_type=MESH)

    def copy3(d, slot):
        return pltpu.make_async_remote_copy(
            grads.at[slot], grads.at[slot], g_send.at[d], g_recv.at[slot],
            device_id=other(d), device_id_type=MESH)

    def send_mode_gram():
        s_hi, s_lo = split(modes[...])
        two = dot(jnp.concatenate([s_hi, s_lo], axis=0), s_hi, NT)
        low = two[rows:]
        mode_gram = two[:rows] + (low + low.T)
        gram2[...] = jnp.concatenate([mode_gram, mode_gram], axis=1)
        sums1[si] = gram2[mine, :]
        for d in range(1, n_space):
            copy1(d, si).start()

    def send_newton():
        for d in range(1, n_space):
            copy1(d, lax.rem(si + d, n_space)).wait_recv()
        m2 = sums1[0]
        for s in range(1, n_space):
            m2 = m2 + sums1[s]
        both = jnp.concatenate([m2 * slope_gram[mine, :], m2 * slope_gram[below, :]], axis=0)
        u, v = iota((2 * rows, rows), 0), iota((2 * rows, rows), 1)
        take_cols = jnp.where(
            (lax.rem(u, rows) // 2 == v // 2) & (u // rows == lax.rem(v, 2)), 1.0, 0.0)
        u, v = iota((share, 2 * share), 0), iota((share, 2 * share), 1)
        take_rows = jnp.where(
            (lax.rem(v, share) // 2 == u // 2) & (v // share == lax.rem(u, 2)), 1.0, 0.0)
        newton = scale * dot(take_rows, dot(both, take_cols, NN, highest), NN, highest)
        sums2[ti] = jnp.concatenate([newton, jnp.zeros_like(newton)], axis=1)
        for d in range(1, n_tm):
            copy2(d, ti).start()

    ahead = min(AHEAD, chunks)
    gram_at = min(chunks - ahead + 1, chunks - 1)
    newton_at = max(chunks - 2, gram_at)
    waited = 0
    for c in range(ahead):
        solve(c)
    for c in range(chunks):
        if c + ahead < chunks:
            solve(c + ahead)
        need = chunks if c >= gram_at else c + 1
        while waited < need:
            modes_copy(waited, 1 - core).wait_recv()
            waited += 1
        if c == gram_at:
            send_mode_gram()
        if c == newton_at:
            send_newton()
        at = slice(c * CHUNK, (c + 1) * CHUNK)
        s_hi, s_lo = split(modes[:, at])
        fitted = dot(jnp.concatenate([s_hi, s_lo, s_hi], axis=0), b_three, TN)
        misfit = slab[at, :] - fitted
        slab[at, :] = misfit
        m_hi, m_lo = split(misfit)
        two = dot(jnp.concatenate([s_hi, s_lo], axis=0), m_hi, NN)
        moment = moment + ((two[rows:] + dot(s_hi, m_lo, NN)) + two[:rows])

    decay = jnp.sum(moment * slopes[:rows, here], axis=1, keepdims=True)
    turn = jnp.sum(moment * slopes[rows:, here], axis=1, keepdims=True)
    u, v = iota((rows, 2 * rows), 0), iota((rows, 2 * rows), 1)
    picked = jnp.where(lax.rem(v, 2) == 0, decay, turn)
    grads[me] = jnp.sum(jnp.where(u // 2 == v // 2, picked, 0.0), axis=0, keepdims=True)

    def send_grad(d, carry):
        copy3(d, me).start()
        return carry

    def take_grad(d, carry):
        copy3(d, lax.rem(me + d, devices)).wait_recv()
        return carry

    def sent_grad(d, carry):
        copy3(d, me).wait_send()
        return carry

    lax.fori_loop(1, devices, send_grad, 0)
    for d in range(1, n_tm):
        copy2(d, lax.rem(ti + d, n_tm)).wait_recv()
    for j in range(n_tm):
        newton_out[j * share:(j + 1) * share, :] = sums2[j, :, :rows]
    lax.fori_loop(1, devices, take_grad, 0)
    grad_out[...] = jnp.sum(grads[...], axis=0)[:, :rows] * -scale

    for c in range(chunks):
        core_copy(c).wait_send()
        for d in range(1, n_y):
            y_copy(c, d, yi).wait_send()
        modes_copy(c, core).wait_send()
    for d in range(1, n_space):
        copy1(d, si).wait_send()
    for d in range(1, n_tm):
        copy2(d, ti).wait_send()
    lax.fori_loop(1, devices, sent_grad, 0)


def write_out(modes, misfit, grad, newton, modes_out, misfit_out, grad_out, newton_out, sem):
    points = misfit.shape[0]
    pieces = [pl.ds(i * (points // 8), points // 8) for i in range(8)]
    copies = [(misfit.at[p], misfit_out.at[p]) for p in pieces]
    copies += [(modes, modes_out), (newton, newton_out), (grad, grad_out)]
    copies = [pltpu.make_async_copy(a, b, sem.at[i]) for i, (a, b) in enumerate(copies)]
    for copy in copies:
        copy.start()
    for copy in copies:
        copy.wait()


def local(n_space, n_tm, frame_slab, pair_decay_rates, pair_angular_frequencies):
    points, epochs = frame_slab.shape
    pairs = pair_decay_rates.shape[0]
    rows = 2 * pairs
    chunks = points // CHUNK
    n_y = n_tm // 2
    share = rows // n_tm
    hbm = pl.BlockSpec(memory_space=pltpu.HBM)
    vmem = pl.BlockSpec(memory_space=pltpu.VMEM)
    dma = pltpu.SemaphoreType.DMA
    shapes = (
        jax.ShapeDtypeStruct((rows, points), f32),
        jax.ShapeDtypeStruct((points, epochs), f32),
        jax.ShapeDtypeStruct((1, rows), f32),
        jax.ShapeDtypeStruct((rows, rows), f32),
    )
    operands = (frame_slab, pair_decay_rates[None, :], pair_angular_frequencies[None, :])
    results = pl.pallas_call(
        functools.partial(kernel, n_space, n_tm, points * n_space),
        out_shape=shapes,
        in_specs=[hbm] * 3,
        out_specs=(vmem,) * 4,
        scratch_shapes=[
            pltpu.VMEM((1, pairs), f32),
            pltpu.VMEM((1, pairs), f32),
            pltpu.VMEM((rows, epochs * n_tm), f32),
            pltpu.VMEM((2 * rows, epochs * n_tm), f32),
            pltpu.VMEM((rows, points), f32),
            pltpu.VMEM((chunks, rows, HALF), f32),
            pltpu.VMEM((chunks, n_y, rows, HALF), f32),
            pltpu.VMEM((rows, 2 * rows), f32),
            pltpu.VMEM((2 * rows, 2 * rows), f32),
            pltpu.VMEM((n_space, share, 2 * rows), f32),
            pltpu.VMEM((n_tm, share, 2 * rows), f32),
            pltpu.VMEM((n_space * n_tm, 1, 2 * rows), f32),
            dma((chunks,)), dma((2,)),
            dma((chunks,)), dma((chunks,)),
            dma((chunks, n_y)), dma((chunks, n_y)),
            dma((chunks,)), dma((chunks,)),
            dma((n_space,)), dma((n_space,)),
            dma((n_tm,)), dma((n_tm,)),
            dma((n_space * n_tm,)), dma((n_space * n_tm,)),
        ],
        compiler_params=pltpu.CompilerParams(
            collective_id=0, has_side_effects=True, vmem_limit_bytes=48 * 2**20
        ),
    )(*(pltpu.with_memory_space_constraint(x, pltpu.HBM) for x in operands))
    modes, misfit, grad, newton = pl.pallas_call(
        write_out,
        out_shape=shapes,
        in_specs=[vmem] * 4,
        out_specs=(hbm,) * 4,
        scratch_shapes=[dma((12,))],
    )(*results)
    return modes, misfit, grad.reshape(rows), newton


def solution(mesh):
    return jax.shard_map(
        functools.partial(local, mesh.shape["space"], mesh.shape["tm"]),
        mesh=mesh,
        in_specs=(P("space", "tm"), P(), P()),
        out_specs=(P(None, "space"), P("space", "tm"), P(), P()),
        check_vma=False,
    )
```

```python
import functools

import jax
import jax.numpy as jnp
from jax import lax
from jax.experimental import pallas as pl
from jax.experimental.pallas import tpu as pltpu
from jax.sharding import PartitionSpec as P

f32 = jnp.float32
bf16 = jnp.bfloat16
highest = lax.Precision.HIGHEST
NN = (((1,), (0,)), ((), ()))
NT = (((1,), (1,)), ((), ()))
TN = (((0,), (0,)), ((), ()))
MESH = pl.DeviceIdType.MESH
CHUNK = 256
HALF = CHUNK // 2
AHEAD = 4
LAG = 2
BLOCK = 128


def dot(a, b, dims, precision=None):
    return lax.dot_general(a, b, dims, precision=precision, preferred_element_type=f32)


def split(x):
    hi = x.astype(bf16)
    return hi, (x - hi.astype(f32)).astype(bf16)


def iota(shape, dim):
    return lax.broadcasted_iota(jnp.int32, shape, dim)


def cos_sin(x):
    n = jnp.floor(x * 0.6366197723675814 + 0.5)
    r = ((x - n * 1.5703125) - n * 0.0004837512969970703) - n * 7.549789948768648e-08
    z = r * r
    s = r + r * z * (-1.6666654611e-1 + z * (8.3321608736e-3 - z * 1.9515295891e-4))
    c = 1.0 - 0.5 * z + z * z * (
        4.166664568298827e-2 + z * (-1.388731625493765e-3 + z * 2.443315711809948e-5))
    q = n.astype(jnp.int32) & 3
    odd = (q & 1) == 1
    cos, sin = jnp.where(odd, s, c), jnp.where(odd, c, s)
    return (jnp.where((q == 1) | (q == 2), -cos, cos), jnp.where(q >= 2, -sin, sin))


def kernel(
    n_space, n_tm, total_points,
    frame, rates_in, freqs_in,
    modes, slab, grad_out, newton_out,
    rates, freqs, basis, slopes, part, from_core, from_y, gram2, slope_gram, sums1, sums2, grads1, grads2,
    in_sem, par_sem, s1_send, s1_recv, y_send, y_recv, ag_send, ag_recv,
    p1_send, p1_recv, p2_send, p2_recv,
    g1_send, g1_recv, g2_send, g2_recv,
):
    points, epochs = slab.shape
    rows = 2 * rates.shape[1]
    chunks = points // CHUNK
    n_y = n_tm // 2
    total_epochs = epochs * n_tm
    share = rows // n_tm
    si, ti = lax.axis_index("space"), lax.axis_index("tm")
    yi, core = ti // 2, lax.rem(ti, 2)
    sibling = yi * 2 + (1 - core)

    def load(c):
        at = pl.ds(c * CHUNK, CHUNK)
        return pltpu.make_async_copy(frame.at[at], slab.at[at], in_sem.at[c])

    parameters = [pltpu.make_async_copy(rates_in, rates, par_sem.at[0]),
                  pltpu.make_async_copy(freqs_in, freqs, par_sem.at[1])]
    for copy in parameters:
        copy.start()
    for c in range(chunks):
        load(c).start()

    barrier = pltpu.get_barrier_semaphore()
    for d in range(1, n_space):
        pl.semaphore_signal(barrier, inc=1, device_id={"space": lax.rem(si + d, n_space)},
                            device_id_type=MESH)
    for d in range(1, n_tm):
        pl.semaphore_signal(barrier, inc=1, device_id={"tm": lax.rem(ti + d, n_tm)},
                            device_id_type=MESH)

    for copy in parameters:
        copy.wait()
    pair_mask = iota((rows, rows // 2), 0) // 2 == iota((rows, rows // 2), 1)
    rate = jnp.sum(jnp.where(pair_mask, rates[...], 0.0), axis=1, keepdims=True)
    freq = jnp.sum(jnp.where(pair_mask, freqs[...], 0.0), axis=1, keepdims=True)
    lane = iota((rows, BLOCK), 1).astype(f32)
    even = lax.rem(iota((rows, BLOCK), 0), 2) == 0
    fine_t = lane / total_epochs
    coarse_t = lane * (BLOCK / total_epochs)
    fine_e = jnp.exp(rate * fine_t)
    fine_c, fine_s = cos_sin(freq * fine_t)
    fine_c, fine_s = fine_e * fine_c, fine_e * fine_s
    coarse_t = jnp.minimum(coarse_t, 1.0)
    coarse_e = jnp.exp(rate * coarse_t)
    ca, sa = cos_sin(freq * coarse_t)
    ca, sa = coarse_e * ca, coarse_e * sa
    first = jnp.where(even, ca, sa)
    second = jnp.where(even, -sa, ca)
    for b in range(total_epochs // BLOCK):
        basis[:, b * BLOCK:(b + 1) * BLOCK] = (
            first[:, b:b + 1] * fine_c + second[:, b:b + 1] * fine_s
        )
    here = pl.ds(pl.multiple_of(ti * epochs, epochs), epochs)
    b_hi, b_lo = split(basis[:, here])
    b_two = jnp.concatenate([b_hi, b_lo], axis=0)

    gram = dot(basis[...], basis[...], NT, highest)
    eye = (iota((rows, rows), 0) == iota((rows, rows), 1)).astype(f32)
    augmented = jnp.concatenate([gram, eye], axis=1)
    tiles = [augmented[i:i + 8] for i in range(0, rows, 8)]
    row_id = iota((8, 2 * rows), 0)

    def eliminate(k):
        own, o = k // 8, k % 8
        r0, r1 = tiles[own][o:o + 1], tiles[own][o + 1:o + 2]
        a, b = r0[:, k:k + 1], r0[:, k + 1:k + 2]
        c, d = r1[:, k:k + 1], r1[:, k + 1:k + 2]
        scale = 1.0 / (a * d - b * c)
        p0 = (d * r0 - b * r1) * scale
        p1 = (a * r1 - c * r0) * scale
        for i in range(len(tiles)):
            t = tiles[i]
            tiles[i] = t - t[:, k:k + 1] * p0 - t[:, k + 1:k + 2] * p1
        tiles[own] = jnp.where(row_id == o, p0, jnp.where(row_id == o + 1, p1, tiles[own]))

    pl.semaphore_wait(barrier, n_space + n_tm - 2)

    def half(c, who):
        return pl.ds(pl.multiple_of(c * CHUNK + who * HALF, HALF), HALF)

    def core_copy(c):
        return pltpu.make_async_remote_copy(
            part.at[:, half(c, 1 - core)], from_core.at[c], s1_send.at[c], s1_recv.at[c],
            device_id={"tm": sibling}, device_id_type=MESH)

    def y_copy(c, d, slot):
        peer = lax.rem(yi + d, n_y) * 2 + core
        return pltpu.make_async_remote_copy(
            from_y.at[c, slot], from_y.at[c, slot], y_send.at[c, d], y_recv.at[c, slot],
            device_id={"tm": peer}, device_id_type=MESH)

    def modes_copy(c, who):
        at = half(c, who)
        return pltpu.make_async_remote_copy(
            modes.at[:, at], modes.at[:, at], ag_send.at[c], ag_recv.at[c],
            device_id={"tm": sibling}, device_id_type=MESH)

    def pass_on(c):
        core_copy(c).wait_recv()
        from_y[c, yi] = part[:, half(c, core)] + from_core[c]
        for d in range(1, n_y):
            y_copy(c, d, yi).start()

    first2 = jnp.where(even, -sa, ca)
    second2 = jnp.where(even, -ca, -sa)

    def slope_block(b):
        at = slice(b * BLOCK, (b + 1) * BLOCK)
        t = fine_t + b * (BLOCK / total_epochs)
        slopes[:rows, at] = basis[:, at] * t
        slopes[rows:, at] = (first2[:, b:b + 1] * fine_c + second2[:, b:b + 1] * fine_s) * t

    blocks = total_epochs // BLOCK
    for c in range(chunks):
        load(c).wait()
        f_hi, f_lo = split(slab[c * CHUNK:(c + 1) * CHUNK, :])
        two = dot(b_two, f_hi, NT)
        part[:, c * CHUNK:(c + 1) * CHUNK] = (two[rows:] + dot(b_hi, f_lo, NT)) + two[:rows]
        core_copy(c).start()
        for k in range(rows * c // chunks, rows * (c + 1) // chunks, 2):
            eliminate(k)
        for b in range(blocks * c // chunks, blocks * (c + 1) // chunks):
            slope_block(b)
        if c >= LAG:
            pass_on(c - LAG)
    for c in range(max(chunks - LAG, 0), chunks):
        pass_on(c)
    j_hi, j_lo = split(slopes[...])
    cross = dot(j_lo, j_hi, NT)
    slope_gram[...] = dot(j_hi, j_hi, NT) + (cross + cross.T)
    inverse = jnp.concatenate(tiles, axis=0)[:, rows:]

    b_three = jnp.concatenate([b_hi, b_hi, b_lo], axis=0)
    moment = jnp.zeros((rows, epochs), f32)

    def solve(c):
        for d in range(1, n_y):
            y_copy(c, d, lax.rem(yi + d, n_y)).wait_recv()
        total = from_y[c, 0]
        for y in range(1, n_y):
            total = total + from_y[c, y]
        modes[:, half(c, core)] = dot(inverse, total, NN, highest)
        modes_copy(c, core).start()

    mine = pl.ds(pl.multiple_of(ti * share, share), share)
    below = pl.ds(pl.multiple_of(ti * share + rows, share), share)
    scale = 1.0 / (total_points * total_epochs)

    def copy1(d, slot):
        return pltpu.make_async_remote_copy(
            sums1.at[slot], sums1.at[slot], p1_send.at[d], p1_recv.at[slot],
            device_id={"space": lax.rem(si + d, n_space)}, device_id_type=MESH)

    def copy2(d, slot):
        return pltpu.make_async_remote_copy(
            sums2.at[slot], sums2.at[slot], p2_send.at[d], p2_recv.at[slot],
            device_id={"tm": lax.rem(ti + d, n_tm)}, device_id_type=MESH)

    def copy3(d, slot):
        return pltpu.make_async_remote_copy(
            grads1.at[slot], grads1.at[slot], g1_send.at[d], g1_recv.at[slot],
            device_id={"space": lax.rem(si + d, n_space)}, device_id_type=MESH)

    def copy4(d, slot):
        return pltpu.make_async_remote_copy(
            grads2.at[slot], grads2.at[slot], g2_send.at[d], g2_recv.at[slot],
            device_id={"tm": lax.rem(ti + d, n_tm)}, device_id_type=MESH)

    def send_mode_gram():
        s_hi, s_lo = split(modes[...])
        two = dot(jnp.concatenate([s_hi, s_lo], axis=0), s_hi, NT)
        low = two[rows:]
        mode_gram = two[:rows] + (low + low.T)
        gram2[...] = jnp.concatenate([mode_gram, mode_gram], axis=1)
        sums1[si] = gram2[mine, :]
        for d in range(1, n_space):
            copy1(d, si).start()

    def send_newton():
        for d in range(1, n_space):
            copy1(d, lax.rem(si + d, n_space)).wait_recv()
        m2 = sums1[0]
        for s in range(1, n_space):
            m2 = m2 + sums1[s]
        both = jnp.concatenate([m2 * slope_gram[mine, :], m2 * slope_gram[below, :]], axis=0)
        u, v = iota((2 * rows, rows), 0), iota((2 * rows, rows), 1)
        take_cols = jnp.where(
            (lax.rem(u, rows) // 2 == v // 2) & (u // rows == lax.rem(v, 2)), 1.0, 0.0)
        u, v = iota((share, 2 * share), 0), iota((share, 2 * share), 1)
        take_rows = jnp.where(
            (lax.rem(v, share) // 2 == u // 2) & (v // share == lax.rem(u, 2)), 1.0, 0.0)
        newton = scale * dot(take_rows, dot(both, take_cols, NN, highest), NN, highest)
        sums2[ti] = jnp.concatenate([newton, jnp.zeros_like(newton)], axis=1)
        for d in range(1, n_tm):
            copy2(d, ti).start()

    ahead = min(AHEAD, chunks)
    gram_at = min(chunks - ahead + 1, chunks - 1)
    waited = 0
    for c in range(ahead):
        solve(c)
    for c in range(chunks):
        if c + ahead < chunks:
            solve(c + ahead)
        need = chunks if c >= gram_at else c + 1
        while waited < need:
            modes_copy(waited, 1 - core).wait_recv()
            waited += 1
        if c == gram_at:
            send_mode_gram()
        at = slice(c * CHUNK, (c + 1) * CHUNK)
        s_hi, s_lo = split(modes[:, at])
        fitted = dot(jnp.concatenate([s_hi, s_lo, s_hi], axis=0), b_three, TN)
        misfit = slab[at, :] - fitted
        slab[at, :] = misfit
        m_hi, m_lo = split(misfit)
        two = dot(jnp.concatenate([s_hi, s_lo], axis=0), m_hi, NN)
        moment = moment + ((two[rows:] + dot(s_hi, m_lo, NN)) + two[:rows])

    decay = jnp.sum(moment * slopes[:rows, here], axis=1, keepdims=True)
    turn = jnp.sum(moment * slopes[rows:, here], axis=1, keepdims=True)
    u, v = iota((rows, 2 * rows), 0), iota((rows, 2 * rows), 1)
    picked = jnp.where(lax.rem(v, 2) == 0, decay, turn)
    grads1[si] = jnp.sum(jnp.where(u // 2 == v // 2, picked, 0.0), axis=0, keepdims=True)
    for d in range(1, n_space):
        copy3(d, si).start()
    send_newton()
    for d in range(1, n_space):
        copy3(d, lax.rem(si + d, n_space)).wait_recv()
    grads2[ti] = jnp.sum(grads1[...], axis=0)
    for d in range(1, n_tm):
        copy4(d, ti).start()
    for d in range(1, n_tm):
        copy2(d, lax.rem(ti + d, n_tm)).wait_recv()
    for j in range(n_tm):
        newton_out[j * share:(j + 1) * share, :] = sums2[j, :, :rows]
    for d in range(1, n_tm):
        copy4(d, lax.rem(ti + d, n_tm)).wait_recv()
    grad_out[...] = jnp.sum(grads2[...], axis=0)[:, :rows] * -scale

    for c in range(chunks):
        core_copy(c).wait_send()
        for d in range(1, n_y):
            y_copy(c, d, yi).wait_send()
        modes_copy(c, core).wait_send()
    for d in range(1, n_space):
        copy1(d, si).wait_send()
        copy3(d, si).wait_send()
    for d in range(1, n_tm):
        copy2(d, ti).wait_send()
        copy4(d, ti).wait_send()


def local(n_space, n_tm, frame_slab, pair_decay_rates, pair_angular_frequencies):
    points, epochs = frame_slab.shape
    pairs = pair_decay_rates.shape[0]
    rows = 2 * pairs
    chunks = points // CHUNK
    n_y = n_tm // 2
    share = rows // n_tm
    hbm = pl.BlockSpec(memory_space=pltpu.HBM)
    vmem = pl.BlockSpec(memory_space=pltpu.VMEM)
    dma = pltpu.SemaphoreType.DMA
    shapes = (
        jax.ShapeDtypeStruct((rows, points), f32),
        jax.ShapeDtypeStruct((points, epochs), f32),
        jax.ShapeDtypeStruct((1, rows), f32),
        jax.ShapeDtypeStruct((rows, rows), f32),
    )
    operands = (frame_slab, pair_decay_rates[None, :], pair_angular_frequencies[None, :])
    modes, misfit, grad, newton = pl.pallas_call(
        functools.partial(kernel, n_space, n_tm, points * n_space),
        out_shape=shapes,
        in_specs=[hbm] * 3,
        out_specs=(vmem,) * 4,
        scratch_shapes=[
            pltpu.VMEM((1, pairs), f32),
            pltpu.VMEM((1, pairs), f32),
            pltpu.VMEM((rows, epochs * n_tm), f32),
            pltpu.VMEM((2 * rows, epochs * n_tm), f32),
            pltpu.VMEM((rows, points), f32),
            pltpu.VMEM((chunks, rows, HALF), f32),
            pltpu.VMEM((chunks, n_y, rows, HALF), f32),
            pltpu.VMEM((rows, 2 * rows), f32),
            pltpu.VMEM((2 * rows, 2 * rows), f32),
            pltpu.VMEM((n_space, share, 2 * rows), f32),
            pltpu.VMEM((n_tm, share, 2 * rows), f32),
            pltpu.VMEM((n_space, 1, 2 * rows), f32),
            pltpu.VMEM((n_tm, 1, 2 * rows), f32),
            dma((chunks,)), dma((2,)),
            dma((chunks,)), dma((chunks,)),
            dma((chunks, n_y)), dma((chunks, n_y)),
            dma((chunks,)), dma((chunks,)),
            dma((n_space,)), dma((n_space,)),
            dma((n_tm,)), dma((n_tm,)),
            dma((n_space,)), dma((n_space,)),
            dma((n_tm,)), dma((n_tm,)),
        ],
        compiler_params=pltpu.CompilerParams(
            collective_id=0, has_side_effects=True, vmem_limit_bytes=48 * 2**20
        ),
    )(*(pltpu.with_memory_space_constraint(x, pltpu.HBM) for x in operands))
    return modes, misfit, grad.reshape(rows), newton


def solution(mesh):
    return jax.shard_map(
        functools.partial(local, mesh.shape["space"], mesh.shape["tm"]),
        mesh=mesh,
        in_specs=(P("space", "tm"), P(), P()),
        out_specs=(P(None, "space"), P("space", "tm"), P(), P()),
        check_vma=False,
    )
```

```python
import functools

import jax
import jax.numpy as jnp
from jax import lax
from jax.experimental import pallas as pl
from jax.experimental.pallas import tpu as pltpu
from jax.sharding import PartitionSpec as P

f32 = jnp.float32
bf16 = jnp.bfloat16
highest = lax.Precision.HIGHEST
NN = (((1,), (0,)), ((), ()))
NT = (((1,), (1,)), ((), ()))
TN = (((0,), (0,)), ((), ()))
MESH = pl.DeviceIdType.MESH
CHUNK = 256
HALF = CHUNK // 2
AHEAD = 4
LAG = 2
BLOCK = 128


def dot(a, b, dims, precision=None):
    return lax.dot_general(a, b, dims, precision=precision, preferred_element_type=f32)


def split(x):
    hi = x.astype(bf16)
    return hi, (x - hi.astype(f32)).astype(bf16)


def split3(x):
    hi = x.astype(bf16)
    rest = x - hi.astype(f32)
    mid = rest.astype(bf16)
    return hi, mid, (rest - mid.astype(f32)).astype(bf16)


def iota(shape, dim):
    return lax.broadcasted_iota(jnp.int32, shape, dim)


def cos_sin(x):
    n = jnp.floor(x * 0.6366197723675814 + 0.5)
    r = ((x - n * 1.5703125) - n * 0.0004837512969970703) - n * 7.549789948768648e-08
    z = r * r
    s = r + r * z * (-1.6666654611e-1 + z * (8.3321608736e-3 - z * 1.9515295891e-4))
    c = 1.0 - 0.5 * z + z * z * (
        4.166664568298827e-2 + z * (-1.388731625493765e-3 + z * 2.443315711809948e-5))
    q = n.astype(jnp.int32) & 3
    odd = (q & 1) == 1
    cos, sin = jnp.where(odd, s, c), jnp.where(odd, c, s)
    return (jnp.where((q == 1) | (q == 2), -cos, cos), jnp.where(q >= 2, -sin, sin))


def kernel(
    n_space, n_tm, total_points,
    frame, rates_in, freqs_in,
    modes, slab, grad_out, newton_out,
    rates, freqs, basis, slopes, part, from_core, from_y, gram2, slope_gram, sums1, sums2, grads1, grads2,
    in_sem, par_sem, s1_send, s1_recv, y_send, y_recv, ag_send, ag_recv,
    p1_send, p1_recv, p2_send, p2_recv,
    g1_send, g1_recv, g2_send, g2_recv,
):
    points, epochs = slab.shape
    rows = 2 * rates.shape[1]
    chunks = points // CHUNK
    n_y = n_tm // 2
    total_epochs = epochs * n_tm
    share = rows // n_tm
    si, ti = lax.axis_index("space"), lax.axis_index("tm")
    yi, core = ti // 2, lax.rem(ti, 2)
    sibling = yi * 2 + (1 - core)

    def load(c):
        at = pl.ds(c * CHUNK, CHUNK)
        return pltpu.make_async_copy(frame.at[at], slab.at[at], in_sem.at[c])

    parameters = [pltpu.make_async_copy(rates_in, rates, par_sem.at[0]),
                  pltpu.make_async_copy(freqs_in, freqs, par_sem.at[1])]
    for copy in parameters:
        copy.start()
    for c in range(chunks):
        load(c).start()

    barrier = pltpu.get_barrier_semaphore()
    for d in range(1, n_space):
        pl.semaphore_signal(barrier, inc=1, device_id={"space": lax.rem(si + d, n_space)},
                            device_id_type=MESH)
    for d in range(1, n_tm):
        pl.semaphore_signal(barrier, inc=1, device_id={"tm": lax.rem(ti + d, n_tm)},
                            device_id_type=MESH)

    for copy in parameters:
        copy.wait()
    pair_mask = iota((rows, rows // 2), 0) // 2 == iota((rows, rows // 2), 1)
    rate = jnp.sum(jnp.where(pair_mask, rates[...], 0.0), axis=1, keepdims=True)
    freq = jnp.sum(jnp.where(pair_mask, freqs[...], 0.0), axis=1, keepdims=True)
    lane = iota((rows, BLOCK), 1).astype(f32)
    even = lax.rem(iota((rows, BLOCK), 0), 2) == 0
    fine_t = lane / total_epochs
    coarse_t = lane * (BLOCK / total_epochs)
    fine_e = jnp.exp(rate * fine_t)
    fine_c, fine_s = cos_sin(freq * fine_t)
    fine_c, fine_s = fine_e * fine_c, fine_e * fine_s
    coarse_t = jnp.minimum(coarse_t, 1.0)
    coarse_e = jnp.exp(rate * coarse_t)
    ca, sa = cos_sin(freq * coarse_t)
    ca, sa = coarse_e * ca, coarse_e * sa
    first = jnp.where(even, ca, sa)
    second = jnp.where(even, -sa, ca)
    for b in range(total_epochs // BLOCK):
        basis[:, b * BLOCK:(b + 1) * BLOCK] = (
            first[:, b:b + 1] * fine_c + second[:, b:b + 1] * fine_s
        )
    here = pl.ds(pl.multiple_of(ti * epochs, epochs), epochs)
    b_hi, b_lo = split(basis[:, here])
    b_fixed = jnp.concatenate([
        jnp.concatenate([b_hi, b_lo], axis=0),
        jnp.concatenate([b_hi, jnp.zeros_like(b_hi)], axis=0),
    ], axis=1).T

    g1, g2, g3 = split3(basis[...])
    three = dot(jnp.concatenate([g1, g2, g3], axis=0), g1, NT)
    low = (three[rows:2 * rows] + dot(g2, g2, NT) * 0.5) + three[2 * rows:]
    gram = three[:rows] + (low + low.T)
    eye = (iota((rows, rows), 0) == iota((rows, rows), 1)).astype(f32)
    augmented = jnp.concatenate([gram, eye], axis=1)
    tiles = [augmented[i:i + 8] for i in range(0, rows, 8)]
    row_id = iota((8, 2 * rows), 0)

    def eliminate(k):
        own, o = k // 8, k % 8
        r0, r1 = tiles[own][o:o + 1], tiles[own][o + 1:o + 2]
        a, b = r0[:, k:k + 1], r0[:, k + 1:k + 2]
        c, d = r1[:, k:k + 1], r1[:, k + 1:k + 2]
        scale = 1.0 / (a * d - b * c)
        p0 = (d * r0 - b * r1) * scale
        p1 = (a * r1 - c * r0) * scale
        for i in range(len(tiles)):
            t = tiles[i]
            tiles[i] = t - t[:, k:k + 1] * p0 - t[:, k + 1:k + 2] * p1
        tiles[own] = jnp.where(row_id == o, p0, jnp.where(row_id == o + 1, p1, tiles[own]))

    pl.semaphore_wait(barrier, n_space + n_tm - 2)

    def half(c, who):
        return pl.ds(pl.multiple_of(c * CHUNK + who * HALF, HALF), HALF)

    def core_copy(c):
        return pltpu.make_async_remote_copy(
            part.at[:, half(c, 1 - core)], from_core.at[c], s1_send.at[c], s1_recv.at[c],
            device_id={"tm": sibling}, device_id_type=MESH)

    def y_copy(c, d, slot):
        peer = lax.rem(yi + d, n_y) * 2 + core
        return pltpu.make_async_remote_copy(
            from_y.at[c, slot], from_y.at[c, slot], y_send.at[c, d], y_recv.at[c, slot],
            device_id={"tm": peer}, device_id_type=MESH)

    def modes_copy(c, who):
        at = half(c, who)
        return pltpu.make_async_remote_copy(
            modes.at[:, at], modes.at[:, at], ag_send.at[c], ag_recv.at[c],
            device_id={"tm": sibling}, device_id_type=MESH)

    def pass_on(c):
        core_copy(c).wait_recv()
        from_y[c, yi] = part[:, half(c, core)] + from_core[c]
        for d in range(1, n_y):
            y_copy(c, d, yi).start()

    first2 = jnp.where(even, -sa, ca)
    second2 = jnp.where(even, -ca, -sa)

    def slope_block(b):
        at = slice(b * BLOCK, (b + 1) * BLOCK)
        t = fine_t + b * (BLOCK / total_epochs)
        slopes[:rows, at] = basis[:, at] * t
        slopes[rows:, at] = (first2[:, b:b + 1] * fine_c + second2[:, b:b + 1] * fine_s) * t

    blocks = total_epochs // BLOCK
    for c in range(chunks):
        load(c).wait()
        f_hi, f_lo = split(slab[c * CHUNK:(c + 1) * CHUNK, :])
        two = dot(jnp.concatenate([f_hi, f_lo], axis=1), b_fixed, NN).T
        part[:, c * CHUNK:(c + 1) * CHUNK] = two[rows:] + two[:rows]
        core_copy(c).start()
        for k in range(rows * c // chunks, rows * (c + 1) // chunks, 2):
            eliminate(k)
        for b in range(blocks * c // chunks, blocks * (c + 1) // chunks):
            slope_block(b)
        if c >= LAG:
            pass_on(c - LAG)
    for c in range(max(chunks - LAG, 0), chunks):
        pass_on(c)
    j_hi, j_lo = split(slopes[...])
    two = dot(jnp.concatenate([j_hi, j_lo], axis=0), j_hi, NT)
    low = two[2 * rows:]
    slope_gram[...] = two[:2 * rows] + (low + low.T)
    i1, i2, i3 = split3(jnp.concatenate(tiles, axis=0)[:, rows:])
    i_six = jnp.concatenate([i3, i2, i1, i2, i1, i1], axis=1)

    b_three = jnp.concatenate([b_hi, b_hi, b_lo], axis=0)
    moment = jnp.zeros((rows, epochs), f32)

    def solve(c):
        for d in range(1, n_y):
            y_copy(c, d, lax.rem(yi + d, n_y)).wait_recv()
        total = from_y[c, 0]
        for y in range(1, n_y):
            total = total + from_y[c, y]
        p1, p2, p3 = split3(total)
        p_six = jnp.concatenate([p1, p2, p3, p1, p2, p1], axis=0)
        modes[:, half(c, core)] = dot(i_six, p_six, NN)
        modes_copy(c, core).start()

    mine = pl.ds(pl.multiple_of(ti * share, share), share)
    below = pl.ds(pl.multiple_of(ti * share + rows, share), share)
    scale = 1.0 / (total_points * total_epochs)

    def copy1(d, slot):
        return pltpu.make_async_remote_copy(
            sums1.at[slot], sums1.at[slot], p1_send.at[d], p1_recv.at[slot],
            device_id={"space": lax.rem(si + d, n_space)}, device_id_type=MESH)

    def copy2(d, slot):
        return pltpu.make_async_remote_copy(
            sums2.at[slot], sums2.at[slot], p2_send.at[d], p2_recv.at[slot],
            device_id={"tm": lax.rem(ti + d, n_tm)}, device_id_type=MESH)

    def copy3(d, slot):
        return pltpu.make_async_remote_copy(
            grads1.at[slot], grads1.at[slot], g1_send.at[d], g1_recv.at[slot],
            device_id={"space": lax.rem(si + d, n_space)}, device_id_type=MESH)

    def copy4(d, slot):
        return pltpu.make_async_remote_copy(
            grads2.at[slot], grads2.at[slot], g2_send.at[d], g2_recv.at[slot],
            device_id={"tm": lax.rem(ti + d, n_tm)}, device_id_type=MESH)

    def send_mode_gram():
        s_hi, s_lo = split(modes[...])
        two = dot(jnp.concatenate([s_hi, s_lo], axis=0), s_hi, NT)
        low = two[rows:]
        mode_gram = two[:rows] + (low + low.T)
        gram2[...] = jnp.concatenate([mode_gram, mode_gram], axis=1)
        sums1[si] = gram2[mine, :]
        for d in range(1, n_space):
            copy1(d, si).start()

    def send_newton():
        for d in range(1, n_space):
            copy1(d, lax.rem(si + d, n_space)).wait_recv()
        m2 = sums1[0]
        for s in range(1, n_space):
            m2 = m2 + sums1[s]
        both = jnp.concatenate([m2 * slope_gram[mine, :], m2 * slope_gram[below, :]], axis=0)
        u, v = iota((2 * rows, rows), 0), iota((2 * rows, rows), 1)
        take_cols = jnp.where(
            (lax.rem(u, rows) // 2 == v // 2) & (u // rows == lax.rem(v, 2)), 1.0, 0.0)
        u, v = iota((share, 2 * share), 0), iota((share, 2 * share), 1)
        take_rows = jnp.where(
            (lax.rem(v, share) // 2 == u // 2) & (v // share == lax.rem(u, 2)), 1.0, 0.0)
        newton = scale * dot(take_rows, dot(both, take_cols, NN, highest), NN, highest)
        sums2[ti] = jnp.concatenate([newton, jnp.zeros_like(newton)], axis=1)
        for d in range(1, n_tm):
            copy2(d, ti).start()

    ahead = min(AHEAD, chunks)
    gram_at = min(chunks - ahead + 1, chunks - 1)
    waited = 0
    for c in range(ahead):
        solve(c)
    for c in range(chunks):
        if c + ahead < chunks:
            solve(c + ahead)
        need = chunks if c >= gram_at else c + 1
        while waited < need:
            modes_copy(waited, 1 - core).wait_recv()
            waited += 1
        if c == gram_at:
            send_mode_gram()
        at = slice(c * CHUNK, (c + 1) * CHUNK)
        s_hi, s_lo = split(modes[:, at])
        fitted = dot(jnp.concatenate([s_hi, s_lo, s_hi], axis=0), b_three, TN)
        misfit = slab[at, :] - fitted
        slab[at, :] = misfit
        m_hi, m_lo = split(misfit)
        two = dot(jnp.concatenate([s_hi, s_lo], axis=0), m_hi, NN)
        moment = moment + ((two[rows:] + dot(s_hi, m_lo, NN)) + two[:rows])

    decay = jnp.sum(moment * slopes[:rows, here], axis=1, keepdims=True)
    turn = jnp.sum(moment * slopes[rows:, here], axis=1, keepdims=True)
    u, v = iota((rows, 2 * rows), 0), iota((rows, 2 * rows), 1)
    picked = jnp.where(lax.rem(v, 2) == 0, decay, turn)
    grads1[si] = jnp.sum(jnp.where(u // 2 == v // 2, picked, 0.0), axis=0, keepdims=True)
    for d in range(1, n_space):
        copy3(d, si).start()
    send_newton()
    for d in range(1, n_space):
        copy3(d, lax.rem(si + d, n_space)).wait_recv()
    grads2[ti] = jnp.sum(grads1[...], axis=0)
    for d in range(1, n_tm):
        copy4(d, ti).start()
    for d in range(1, n_tm):
        copy2(d, lax.rem(ti + d, n_tm)).wait_recv()
    for j in range(n_tm):
        newton_out[j * share:(j + 1) * share, :] = sums2[j, :, :rows]
    for d in range(1, n_tm):
        copy4(d, lax.rem(ti + d, n_tm)).wait_recv()
    grad_out[...] = jnp.sum(grads2[...], axis=0)[:, :rows] * -scale

    for c in range(chunks):
        core_copy(c).wait_send()
        for d in range(1, n_y):
            y_copy(c, d, yi).wait_send()
        modes_copy(c, core).wait_send()
    for d in range(1, n_space):
        copy1(d, si).wait_send()
        copy3(d, si).wait_send()
    for d in range(1, n_tm):
        copy2(d, ti).wait_send()
        copy4(d, ti).wait_send()


def local(n_space, n_tm, frame_slab, pair_decay_rates, pair_angular_frequencies):
    points, epochs = frame_slab.shape
    pairs = pair_decay_rates.shape[0]
    rows = 2 * pairs
    chunks = points // CHUNK
    n_y = n_tm // 2
    share = rows // n_tm
    hbm = pl.BlockSpec(memory_space=pltpu.HBM)
    vmem = pl.BlockSpec(memory_space=pltpu.VMEM)
    dma = pltpu.SemaphoreType.DMA
    shapes = (
        jax.ShapeDtypeStruct((rows, points), f32),
        jax.ShapeDtypeStruct((points, epochs), f32),
        jax.ShapeDtypeStruct((1, rows), f32),
        jax.ShapeDtypeStruct((rows, rows), f32),
    )
    operands = (frame_slab, pair_decay_rates[None, :], pair_angular_frequencies[None, :])
    modes, misfit, grad, newton = pl.pallas_call(
        functools.partial(kernel, n_space, n_tm, points * n_space),
        out_shape=shapes,
        in_specs=[hbm] * 3,
        out_specs=(vmem,) * 4,
        scratch_shapes=[
            pltpu.VMEM((1, pairs), f32),
            pltpu.VMEM((1, pairs), f32),
            pltpu.VMEM((rows, epochs * n_tm), f32),
            pltpu.VMEM((2 * rows, epochs * n_tm), f32),
            pltpu.VMEM((rows, points), f32),
            pltpu.VMEM((chunks, rows, HALF), f32),
            pltpu.VMEM((chunks, n_y, rows, HALF), f32),
            pltpu.VMEM((rows, 2 * rows), f32),
            pltpu.VMEM((2 * rows, 2 * rows), f32),
            pltpu.VMEM((n_space, share, 2 * rows), f32),
            pltpu.VMEM((n_tm, share, 2 * rows), f32),
            pltpu.VMEM((n_space, 1, 2 * rows), f32),
            pltpu.VMEM((n_tm, 1, 2 * rows), f32),
            dma((chunks,)), dma((2,)),
            dma((chunks,)), dma((chunks,)),
            dma((chunks, n_y)), dma((chunks, n_y)),
            dma((chunks,)), dma((chunks,)),
            dma((n_space,)), dma((n_space,)),
            dma((n_tm,)), dma((n_tm,)),
            dma((n_space,)), dma((n_space,)),
            dma((n_tm,)), dma((n_tm,)),
        ],
        compiler_params=pltpu.CompilerParams(
            collective_id=0, has_side_effects=True, vmem_limit_bytes=48 * 2**20
        ),
    )(*(pltpu.with_memory_space_constraint(x, pltpu.HBM) for x in operands))
    return modes, misfit, grad.reshape(rows), newton


def solution(mesh):
    return jax.shard_map(
        functools.partial(local, mesh.shape["space"], mesh.shape["tm"]),
        mesh=mesh,
        in_specs=(P("space", "tm"), P(), P()),
        out_specs=(P(None, "space"), P("space", "tm"), P(), P()),
        check_vma=False,
    )
```

```python
import functools

import jax
import jax.numpy as jnp
from jax import lax
from jax.experimental import pallas as pl
from jax.experimental.pallas import tpu as pltpu
from jax.sharding import PartitionSpec as P

f32 = jnp.float32
bf16 = jnp.bfloat16
highest = lax.Precision.HIGHEST
NN = (((1,), (0,)), ((), ()))
NT = (((1,), (1,)), ((), ()))
TN = (((0,), (0,)), ((), ()))
MESH = pl.DeviceIdType.MESH
CHUNK = 256
HALF = CHUNK // 2
AHEAD = 4
LAG = 2
BLOCK = 128


def dot(a, b, dims, precision=None):
    return lax.dot_general(a, b, dims, precision=precision, preferred_element_type=f32)


def split(x):
    hi = x.astype(bf16)
    return hi, (x - hi.astype(f32)).astype(bf16)


def split3(x):
    hi = x.astype(bf16)
    rest = x - hi.astype(f32)
    mid = rest.astype(bf16)
    return hi, mid, (rest - mid.astype(f32)).astype(bf16)


def iota(shape, dim):
    return lax.broadcasted_iota(jnp.int32, shape, dim)


def cos_sin(x):
    n = jnp.floor(x * 0.6366197723675814 + 0.5)
    r = ((x - n * 1.5703125) - n * 0.0004837512969970703) - n * 7.549789948768648e-08
    z = r * r
    s = r + r * z * (-1.6666654611e-1 + z * (8.3321608736e-3 - z * 1.9515295891e-4))
    c = 1.0 - 0.5 * z + z * z * (
        4.166664568298827e-2 + z * (-1.388731625493765e-3 + z * 2.443315711809948e-5))
    q = n.astype(jnp.int32) & 3
    odd = (q & 1) == 1
    cos, sin = jnp.where(odd, s, c), jnp.where(odd, c, s)
    return (jnp.where((q == 1) | (q == 2), -cos, cos), jnp.where(q >= 2, -sin, sin))


def kernel(
    n_space, n_tm, total_points,
    frame, rates_in, freqs_in,
    modes, slab, grad_out, newton_out,
    rates, freqs, basis, slopes, part, from_core, from_y, gram2, slope_gram, sums1, sums2, grads1, grads2,
    in_sem, par_sem, s1_send, s1_recv, y_send, y_recv, ag_send, ag_recv,
    p1_send, p1_recv, p2_send, p2_recv,
    g1_send, g1_recv, g2_send, g2_recv,
):
    points, epochs = slab.shape
    rows = 2 * rates.shape[1]
    chunks = points // CHUNK
    n_y = n_tm // 2
    total_epochs = epochs * n_tm
    share = rows // n_tm
    si, ti = lax.axis_index("space"), lax.axis_index("tm")
    yi, core = ti // 2, lax.rem(ti, 2)
    sibling = yi * 2 + (1 - core)

    def load(c):
        at = pl.ds(c * CHUNK, CHUNK)
        return pltpu.make_async_copy(frame.at[at], slab.at[at], in_sem.at[c])

    parameters = [pltpu.make_async_copy(rates_in, rates, par_sem.at[0]),
                  pltpu.make_async_copy(freqs_in, freqs, par_sem.at[1])]
    for copy in parameters:
        copy.start()
    for c in range(chunks):
        load(c).start()

    barrier = pltpu.get_barrier_semaphore()
    for d in range(1, n_space):
        pl.semaphore_signal(barrier, inc=1, device_id={"space": lax.rem(si + d, n_space)},
                            device_id_type=MESH)
    for d in range(1, n_tm):
        pl.semaphore_signal(barrier, inc=1, device_id={"tm": lax.rem(ti + d, n_tm)},
                            device_id_type=MESH)

    for copy in parameters:
        copy.wait()
    pair_mask = iota((rows, rows // 2), 0) // 2 == iota((rows, rows // 2), 1)
    rate = jnp.sum(jnp.where(pair_mask, rates[...], 0.0), axis=1, keepdims=True)
    freq = jnp.sum(jnp.where(pair_mask, freqs[...], 0.0), axis=1, keepdims=True)
    lane = iota((rows, BLOCK), 1).astype(f32)
    even = lax.rem(iota((rows, BLOCK), 0), 2) == 0
    fine_t = lane / total_epochs
    coarse_t = lane * (BLOCK / total_epochs)
    fine_e = jnp.exp(rate * fine_t)
    fine_c, fine_s = cos_sin(freq * fine_t)
    fine_c, fine_s = fine_e * fine_c, fine_e * fine_s
    coarse_t = jnp.minimum(coarse_t, 1.0)
    coarse_e = jnp.exp(rate * coarse_t)
    ca, sa = cos_sin(freq * coarse_t)
    ca, sa = coarse_e * ca, coarse_e * sa
    first = jnp.where(even, ca, sa)
    second = jnp.where(even, -sa, ca)
    for b in range(total_epochs // BLOCK):
        basis[:, b * BLOCK:(b + 1) * BLOCK] = (
            first[:, b:b + 1] * fine_c + second[:, b:b + 1] * fine_s
        )
    here = pl.ds(pl.multiple_of(ti * epochs, epochs), epochs)
    b_hi, b_lo = split(basis[:, here])
    b_fixed = jnp.concatenate([
        jnp.concatenate([b_hi, b_lo], axis=0),
        jnp.concatenate([b_hi, jnp.zeros_like(b_hi)], axis=0),
    ], axis=1).T

    g1, g2, g3 = split3(basis[...])
    three = dot(jnp.concatenate([g1, g2, g3], axis=0), g1, NT)
    low = (three[rows:2 * rows] + dot(g2, g2, NT) * 0.5) + three[2 * rows:]
    gram = three[:rows] + (low + low.T)
    eye = (iota((rows, rows), 0) == iota((rows, rows), 1)).astype(f32)
    augmented = jnp.concatenate([gram, eye], axis=1)
    tiles = [augmented[i:i + 8] for i in range(0, rows, 8)]
    row_id = iota((8, 2 * rows), 0)

    def eliminate(k):
        own, o = k // 8, k % 8
        full = (8, 2 * rows)
        t = tiles[own]
        left = jnp.broadcast_to(t[:, k:k + 1], full)
        right = jnp.broadcast_to(t[:, k + 1:k + 2], full)
        a, c = (jnp.broadcast_to(left[i:i + 1], full) for i in (o, o + 1))
        b, d = (jnp.broadcast_to(right[i:i + 1], full) for i in (o, o + 1))
        r0, r1 = (jnp.broadcast_to(t[i:i + 1], full) for i in (o, o + 1))
        scale = 1.0 / (a * d - b * c)
        p0 = (d * r0 - b * r1) * scale
        p1 = (a * r1 - c * r0) * scale
        for i in range(len(tiles)):
            if i != own:
                u = tiles[i]
                tiles[i] = u - u[:, k:k + 1] * p0 - u[:, k + 1:k + 2] * p1
        tiles[own] = jnp.where(
            row_id == o, p0, jnp.where(row_id == o + 1, p1, t - left * p0 - right * p1))

    pl.semaphore_wait(barrier, n_space + n_tm - 2)

    def half(c, who):
        return pl.ds(pl.multiple_of(c * CHUNK + who * HALF, HALF), HALF)

    def core_copy(c):
        return pltpu.make_async_remote_copy(
            part.at[:, half(c, 1 - core)], from_core.at[c], s1_send.at[c], s1_recv.at[c],
            device_id={"tm": sibling}, device_id_type=MESH)

    def y_copy(c, d, slot):
        peer = lax.rem(yi + d, n_y) * 2 + core
        return pltpu.make_async_remote_copy(
            from_y.at[c, slot], from_y.at[c, slot], y_send.at[c, d], y_recv.at[c, slot],
            device_id={"tm": peer}, device_id_type=MESH)

    def modes_copy(c, who):
        at = half(c, who)
        return pltpu.make_async_remote_copy(
            modes.at[:, at], modes.at[:, at], ag_send.at[c], ag_recv.at[c],
            device_id={"tm": sibling}, device_id_type=MESH)

    def pass_on(c):
        core_copy(c).wait_recv()
        from_y[c, yi] = part[:, half(c, core)] + from_core[c]
        for d in range(1, n_y):
            y_copy(c, d, yi).start()

    first2 = jnp.where(even, -sa, ca)
    second2 = jnp.where(even, -ca, -sa)

    def slope_block(b):
        at = slice(b * BLOCK, (b + 1) * BLOCK)
        t = fine_t + b * (BLOCK / total_epochs)
        slopes[:rows, at] = basis[:, at] * t
        slopes[rows:, at] = (first2[:, b:b + 1] * fine_c + second2[:, b:b + 1] * fine_s) * t

    blocks = total_epochs // BLOCK
    for c in range(chunks):
        load(c).wait()
        f_hi, f_lo = split(slab[c * CHUNK:(c + 1) * CHUNK, :])
        two = dot(jnp.concatenate([f_hi, f_lo], axis=1), b_fixed, NN).T
        part[:, c * CHUNK:(c + 1) * CHUNK] = two[rows:] + two[:rows]
        core_copy(c).start()
        for k in range(rows * c // chunks, rows * (c + 1) // chunks, 2):
            eliminate(k)
        for b in range(blocks * c // chunks, blocks * (c + 1) // chunks):
            slope_block(b)
        if c >= LAG:
            pass_on(c - LAG)
    for c in range(max(chunks - LAG, 0), chunks):
        pass_on(c)
    j_hi, j_lo = split(slopes[...])
    two = dot(jnp.concatenate([j_hi, j_lo], axis=0), j_hi, NT)
    low = two[2 * rows:]
    slope_gram[...] = two[:2 * rows] + (low + low.T)
    i1, i2, i3 = split3(jnp.concatenate(tiles, axis=0)[:, rows:])
    i_six = jnp.concatenate([i3, i2, i1, i2, i1, i1], axis=1)

    b_three = jnp.concatenate([b_hi, b_hi, b_lo], axis=0)
    moment = jnp.zeros((rows, epochs), f32)

    def solve(c):
        for d in range(1, n_y):
            y_copy(c, d, lax.rem(yi + d, n_y)).wait_recv()
        total = from_y[c, 0]
        for y in range(1, n_y):
            total = total + from_y[c, y]
        p1, p2, p3 = split3(total)
        p_six = jnp.concatenate([p1, p2, p3, p1, p2, p1], axis=0)
        modes[:, half(c, core)] = dot(i_six, p_six, NN)
        modes_copy(c, core).start()

    mine = pl.ds(pl.multiple_of(ti * share, share), share)
    below = pl.ds(pl.multiple_of(ti * share + rows, share), share)
    scale = 1.0 / (total_points * total_epochs)

    def copy1(d, slot):
        return pltpu.make_async_remote_copy(
            sums1.at[slot], sums1.at[slot], p1_send.at[d], p1_recv.at[slot],
            device_id={"space": lax.rem(si + d, n_space)}, device_id_type=MESH)

    def copy2(d, slot):
        return pltpu.make_async_remote_copy(
            sums2.at[slot], sums2.at[slot], p2_send.at[d], p2_recv.at[slot],
            device_id={"tm": lax.rem(ti + d, n_tm)}, device_id_type=MESH)

    def copy3(d, slot):
        return pltpu.make_async_remote_copy(
            grads1.at[slot], grads1.at[slot], g1_send.at[d], g1_recv.at[slot],
            device_id={"space": lax.rem(si + d, n_space)}, device_id_type=MESH)

    def copy4(d, slot):
        return pltpu.make_async_remote_copy(
            grads2.at[slot], grads2.at[slot], g2_send.at[d], g2_recv.at[slot],
            device_id={"tm": lax.rem(ti + d, n_tm)}, device_id_type=MESH)

    def send_mode_gram():
        s_hi, s_lo = split(modes[...])
        two = dot(jnp.concatenate([s_hi, s_lo], axis=0), s_hi, NT)
        low = two[rows:]
        mode_gram = two[:rows] + (low + low.T)
        gram2[...] = jnp.concatenate([mode_gram, mode_gram], axis=1)
        sums1[si] = gram2[mine, :]
        for d in range(1, n_space):
            copy1(d, si).start()

    def send_newton():
        for d in range(1, n_space):
            copy1(d, lax.rem(si + d, n_space)).wait_recv()
        m2 = sums1[0]
        for s in range(1, n_space):
            m2 = m2 + sums1[s]
        both = jnp.concatenate([m2 * slope_gram[mine, :], m2 * slope_gram[below, :]], axis=0)
        u, v = iota((2 * rows, rows), 0), iota((2 * rows, rows), 1)
        take_cols = jnp.where(
            (lax.rem(u, rows) // 2 == v // 2) & (u // rows == lax.rem(v, 2)), 1.0, 0.0)
        u, v = iota((share, 2 * share), 0), iota((share, 2 * share), 1)
        take_rows = jnp.where(
            (lax.rem(v, share) // 2 == u // 2) & (v // share == lax.rem(u, 2)), 1.0, 0.0)
        newton = scale * dot(take_rows, dot(both, take_cols, NN, highest), NN, highest)
        sums2[ti] = jnp.concatenate([newton, jnp.zeros_like(newton)], axis=1)
        for d in range(1, n_tm):
            copy2(d, ti).start()

    ahead = min(AHEAD, chunks)
    gram_at = min(chunks - ahead + 1, chunks - 1)
    waited = 0
    for c in range(ahead):
        solve(c)
    for c in range(chunks):
        if c + ahead < chunks:
            solve(c + ahead)
        need = chunks if c >= gram_at else c + 1
        while waited < need:
            modes_copy(waited, 1 - core).wait_recv()
            waited += 1
        if c == gram_at:
            send_mode_gram()
        at = slice(c * CHUNK, (c + 1) * CHUNK)
        s_hi, s_lo = split(modes[:, at])
        fitted = dot(jnp.concatenate([s_hi, s_lo, s_hi], axis=0), b_three, TN)
        misfit = slab[at, :] - fitted
        slab[at, :] = misfit
        m_hi, m_lo = split(misfit)
        two = dot(jnp.concatenate([s_hi, s_lo], axis=0), m_hi, NN)
        moment = moment + ((two[rows:] + dot(s_hi, m_lo, NN)) + two[:rows])

    decay = jnp.sum(moment * slopes[:rows, here], axis=1, keepdims=True)
    turn = jnp.sum(moment * slopes[rows:, here], axis=1, keepdims=True)
    u, v = iota((rows, 2 * rows), 0), iota((rows, 2 * rows), 1)
    picked = jnp.where(lax.rem(v, 2) == 0, decay, turn)
    grads1[si] = jnp.sum(jnp.where(u // 2 == v // 2, picked, 0.0), axis=0, keepdims=True)
    for d in range(1, n_space):
        copy3(d, si).start()
    send_newton()
    for d in range(1, n_space):
        copy3(d, lax.rem(si + d, n_space)).wait_recv()
    grads2[ti] = jnp.sum(grads1[...], axis=0)
    for d in range(1, n_tm):
        copy4(d, ti).start()
    for d in range(1, n_tm):
        copy2(d, lax.rem(ti + d, n_tm)).wait_recv()
    for j in range(n_tm):
        newton_out[j * share:(j + 1) * share, :] = sums2[j, :, :rows]
    for d in range(1, n_tm):
        copy4(d, lax.rem(ti + d, n_tm)).wait_recv()
    grad_out[...] = jnp.sum(grads2[...], axis=0)[:, :rows] * -scale

    for c in range(chunks):
        core_copy(c).wait_send()
        for d in range(1, n_y):
            y_copy(c, d, yi).wait_send()
        modes_copy(c, core).wait_send()
    for d in range(1, n_space):
        copy1(d, si).wait_send()
        copy3(d, si).wait_send()
    for d in range(1, n_tm):
        copy2(d, ti).wait_send()
        copy4(d, ti).wait_send()


def local(n_space, n_tm, frame_slab, pair_decay_rates, pair_angular_frequencies):
    points, epochs = frame_slab.shape
    pairs = pair_decay_rates.shape[0]
    rows = 2 * pairs
    chunks = points // CHUNK
    n_y = n_tm // 2
    share = rows // n_tm
    hbm = pl.BlockSpec(memory_space=pltpu.HBM)
    vmem = pl.BlockSpec(memory_space=pltpu.VMEM)
    dma = pltpu.SemaphoreType.DMA
    shapes = (
        jax.ShapeDtypeStruct((rows, points), f32),
        jax.ShapeDtypeStruct((points, epochs), f32),
        jax.ShapeDtypeStruct((1, rows), f32),
        jax.ShapeDtypeStruct((rows, rows), f32),
    )
    operands = (frame_slab, pair_decay_rates[None, :], pair_angular_frequencies[None, :])
    modes, misfit, grad, newton = pl.pallas_call(
        functools.partial(kernel, n_space, n_tm, points * n_space),
        out_shape=shapes,
        in_specs=[hbm] * 3,
        out_specs=(vmem,) * 4,
        scratch_shapes=[
            pltpu.VMEM((1, pairs), f32),
            pltpu.VMEM((1, pairs), f32),
            pltpu.VMEM((rows, epochs * n_tm), f32),
            pltpu.VMEM((2 * rows, epochs * n_tm), f32),
            pltpu.VMEM((rows, points), f32),
            pltpu.VMEM((chunks, rows, HALF), f32),
            pltpu.VMEM((chunks, n_y, rows, HALF), f32),
            pltpu.VMEM((rows, 2 * rows), f32),
            pltpu.VMEM((2 * rows, 2 * rows), f32),
            pltpu.VMEM((n_space, share, 2 * rows), f32),
            pltpu.VMEM((n_tm, share, 2 * rows), f32),
            pltpu.VMEM((n_space, 1, 2 * rows), f32),
            pltpu.VMEM((n_tm, 1, 2 * rows), f32),
            dma((chunks,)), dma((2,)),
            dma((chunks,)), dma((chunks,)),
            dma((chunks, n_y)), dma((chunks, n_y)),
            dma((chunks,)), dma((chunks,)),
            dma((n_space,)), dma((n_space,)),
            dma((n_tm,)), dma((n_tm,)),
            dma((n_space,)), dma((n_space,)),
            dma((n_tm,)), dma((n_tm,)),
        ],
        compiler_params=pltpu.CompilerParams(
            collective_id=0, has_side_effects=True, vmem_limit_bytes=48 * 2**20
        ),
    )(*(pltpu.with_memory_space_constraint(x, pltpu.HBM) for x in operands))
    return modes, misfit, grad.reshape(rows), newton


def solution(mesh):
    return jax.shard_map(
        functools.partial(local, mesh.shape["space"], mesh.shape["tm"]),
        mesh=mesh,
        in_specs=(P("space", "tm"), P(), P()),
        out_specs=(P(None, "space"), P("space", "tm"), P(), P()),
        check_vma=False,
    )
```

```python
import functools

import jax
import jax.numpy as jnp
from jax import lax
from jax.experimental import pallas as pl
from jax.experimental.pallas import tpu as pltpu
from jax.sharding import PartitionSpec as P

f32 = jnp.float32
bf16 = jnp.bfloat16
highest = lax.Precision.HIGHEST
NN = (((1,), (0,)), ((), ()))
NT = (((1,), (1,)), ((), ()))
TN = (((0,), (0,)), ((), ()))
MESH = pl.DeviceIdType.MESH
CHUNK = 512
HALF = CHUNK // 2
AHEAD = 3
LAG = 1
BLOCK = 128


def dot(a, b, dims, precision=None):
    return lax.dot_general(a, b, dims, precision=precision, preferred_element_type=f32)


def split(x):
    hi = x.astype(bf16)
    return hi, (x - hi.astype(f32)).astype(bf16)


def split3(x):
    hi = x.astype(bf16)
    rest = x - hi.astype(f32)
    mid = rest.astype(bf16)
    return hi, mid, (rest - mid.astype(f32)).astype(bf16)


def iota(shape, dim):
    return lax.broadcasted_iota(jnp.int32, shape, dim)


def cos_sin(x):
    n = jnp.floor(x * 0.6366197723675814 + 0.5)
    r = ((x - n * 1.5703125) - n * 0.0004837512969970703) - n * 7.549789948768648e-08
    z = r * r
    s = r + r * z * (-1.6666654611e-1 + z * (8.3321608736e-3 - z * 1.9515295891e-4))
    c = 1.0 - 0.5 * z + z * z * (
        4.166664568298827e-2 + z * (-1.388731625493765e-3 + z * 2.443315711809948e-5))
    q = n.astype(jnp.int32) & 3
    odd = (q & 1) == 1
    cos, sin = jnp.where(odd, s, c), jnp.where(odd, c, s)
    return (jnp.where((q == 1) | (q == 2), -cos, cos), jnp.where(q >= 2, -sin, sin))


def kernel(
    n_space, n_tm, total_points,
    frame, rates_in, freqs_in,
    modes, slab, grad_out, newton_out,
    rates, freqs, basis, slopes, part, from_core, from_y, gram2, slope_gram, sums1, sums2, grads1, grads2,
    in_sem, par_sem, s1_send, s1_recv, y_send, y_recv, ag_send, ag_recv,
    p1_send, p1_recv, p2_send, p2_recv,
    g1_send, g1_recv, g2_send, g2_recv,
):
    points, epochs = slab.shape
    rows = 2 * rates.shape[1]
    chunks = points // CHUNK
    n_y = n_tm // 2
    total_epochs = epochs * n_tm
    share = rows // n_tm
    si, ti = lax.axis_index("space"), lax.axis_index("tm")
    yi, core = ti // 2, lax.rem(ti, 2)
    sibling = yi * 2 + (1 - core)

    def load(c):
        at = pl.ds(c * CHUNK, CHUNK)
        return pltpu.make_async_copy(frame.at[at], slab.at[at], in_sem.at[c])

    parameters = [pltpu.make_async_copy(rates_in, rates, par_sem.at[0]),
                  pltpu.make_async_copy(freqs_in, freqs, par_sem.at[1])]
    for copy in parameters:
        copy.start()
    for c in range(chunks):
        load(c).start()

    barrier = pltpu.get_barrier_semaphore()
    for d in range(1, n_space):
        pl.semaphore_signal(barrier, inc=1, device_id={"space": lax.rem(si + d, n_space)},
                            device_id_type=MESH)
    for d in range(1, n_tm):
        pl.semaphore_signal(barrier, inc=1, device_id={"tm": lax.rem(ti + d, n_tm)},
                            device_id_type=MESH)

    for copy in parameters:
        copy.wait()
    pair_mask = iota((rows, rows // 2), 0) // 2 == iota((rows, rows // 2), 1)
    rate = jnp.sum(jnp.where(pair_mask, rates[...], 0.0), axis=1, keepdims=True)
    freq = jnp.sum(jnp.where(pair_mask, freqs[...], 0.0), axis=1, keepdims=True)
    lane = iota((rows, BLOCK), 1).astype(f32)
    even = lax.rem(iota((rows, BLOCK), 0), 2) == 0
    fine_t = lane / total_epochs
    coarse_t = lane * (BLOCK / total_epochs)
    fine_e = jnp.exp(rate * fine_t)
    fine_c, fine_s = cos_sin(freq * fine_t)
    fine_c, fine_s = fine_e * fine_c, fine_e * fine_s
    coarse_t = jnp.minimum(coarse_t, 1.0)
    coarse_e = jnp.exp(rate * coarse_t)
    ca, sa = cos_sin(freq * coarse_t)
    ca, sa = coarse_e * ca, coarse_e * sa
    first = jnp.where(even, ca, sa)
    second = jnp.where(even, -sa, ca)
    for b in range(total_epochs // BLOCK):
        basis[:, b * BLOCK:(b + 1) * BLOCK] = (
            first[:, b:b + 1] * fine_c + second[:, b:b + 1] * fine_s
        )
    here = pl.ds(pl.multiple_of(ti * epochs, epochs), epochs)
    b_hi, b_lo = split(basis[:, here])
    b_fixed = jnp.concatenate([
        jnp.concatenate([b_hi, b_lo], axis=0),
        jnp.concatenate([b_hi, jnp.zeros_like(b_hi)], axis=0),
    ], axis=1).T

    g1, g2, g3 = split3(basis[...])
    three = dot(jnp.concatenate([g1, g2, g3], axis=0), g1, NT)
    low = (three[rows:2 * rows] + dot(g2, g2, NT) * 0.5) + three[2 * rows:]
    gram = three[:rows] + (low + low.T)
    eye = (iota((rows, rows), 0) == iota((rows, rows), 1)).astype(f32)
    augmented = jnp.concatenate([gram, eye], axis=1)
    tiles = [augmented[i:i + 8] for i in range(0, rows, 8)]
    row_id = iota((8, 2 * rows), 0)

    def eliminate(k):
        own, o = k // 8, k % 8
        full = (8, 2 * rows)
        t = tiles[own]
        left = jnp.broadcast_to(t[:, k:k + 1], full)
        right = jnp.broadcast_to(t[:, k + 1:k + 2], full)
        a, c = (jnp.broadcast_to(left[i:i + 1], full) for i in (o, o + 1))
        b, d = (jnp.broadcast_to(right[i:i + 1], full) for i in (o, o + 1))
        r0, r1 = (jnp.broadcast_to(t[i:i + 1], full) for i in (o, o + 1))
        scale = 1.0 / (a * d - b * c)
        p0 = (d * r0 - b * r1) * scale
        p1 = (a * r1 - c * r0) * scale
        for i in range(len(tiles)):
            if i != own:
                u = tiles[i]
                tiles[i] = u - u[:, k:k + 1] * p0 - u[:, k + 1:k + 2] * p1
        tiles[own] = jnp.where(
            row_id == o, p0, jnp.where(row_id == o + 1, p1, t - left * p0 - right * p1))

    pl.semaphore_wait(barrier, n_space + n_tm - 2)

    def half(c, who):
        return pl.ds(pl.multiple_of(c * CHUNK + who * HALF, HALF), HALF)

    def core_copy(c):
        return pltpu.make_async_remote_copy(
            part.at[:, half(c, 1 - core)], from_core.at[c], s1_send.at[c], s1_recv.at[c],
            device_id={"tm": sibling}, device_id_type=MESH)

    def y_copy(c, d, slot):
        peer = lax.rem(yi + d, n_y) * 2 + core
        return pltpu.make_async_remote_copy(
            from_y.at[c, slot], from_y.at[c, slot], y_send.at[c, d], y_recv.at[c, slot],
            device_id={"tm": peer}, device_id_type=MESH)

    def modes_copy(c, who):
        at = half(c, who)
        return pltpu.make_async_remote_copy(
            modes.at[:, at], modes.at[:, at], ag_send.at[c], ag_recv.at[c],
            device_id={"tm": sibling}, device_id_type=MESH)

    def pass_on(c):
        core_copy(c).wait_recv()
        from_y[c, yi] = part[:, half(c, core)] + from_core[c]
        for d in range(1, n_y):
            y_copy(c, d, yi).start()

    first2 = jnp.where(even, -sa, ca)
    second2 = jnp.where(even, -ca, -sa)

    def slope_block(b):
        at = slice(b * BLOCK, (b + 1) * BLOCK)
        t = fine_t + b * (BLOCK / total_epochs)
        slopes[:rows, at] = basis[:, at] * t
        slopes[rows:, at] = (first2[:, b:b + 1] * fine_c + second2[:, b:b + 1] * fine_s) * t

    blocks = total_epochs // BLOCK
    for c in range(chunks):
        load(c).wait()
        f_hi, f_lo = split(slab[c * CHUNK:(c + 1) * CHUNK, :])
        two = dot(jnp.concatenate([f_hi, f_lo], axis=1), b_fixed, NN).T
        part[:, c * CHUNK:(c + 1) * CHUNK] = two[rows:] + two[:rows]
        core_copy(c).start()
        for k in range(rows * c // chunks, rows * (c + 1) // chunks, 2):
            eliminate(k)
        for b in range(blocks * c // chunks, blocks * (c + 1) // chunks):
            slope_block(b)
        if c >= LAG:
            pass_on(c - LAG)
    for c in range(max(chunks - LAG, 0), chunks):
        pass_on(c)
    j_hi, j_lo = split(slopes[...])
    two = dot(jnp.concatenate([j_hi, j_lo], axis=0), j_hi, NT)
    low = two[2 * rows:]
    slope_gram[...] = two[:2 * rows] + (low + low.T)
    i1, i2, i3 = split3(jnp.concatenate(tiles, axis=0)[:, rows:])
    i_six = jnp.concatenate([i3, i2, i1, i2, i1, i1], axis=1)

    b_three = jnp.concatenate([b_hi, b_hi, b_lo], axis=0)
    moment = jnp.zeros((rows, epochs), f32)

    def solve(c):
        for d in range(1, n_y):
            y_copy(c, d, lax.rem(yi + d, n_y)).wait_recv()
        total = from_y[c, 0]
        for y in range(1, n_y):
            total = total + from_y[c, y]
        p1, p2, p3 = split3(total)
        p_six = jnp.concatenate([p1, p2, p3, p1, p2, p1], axis=0)
        modes[:, half(c, core)] = dot(i_six, p_six, NN)
        modes_copy(c, core).start()

    mine = pl.ds(pl.multiple_of(ti * share, share), share)
    below = pl.ds(pl.multiple_of(ti * share + rows, share), share)
    scale = 1.0 / (total_points * total_epochs)

    def copy1(d, slot):
        return pltpu.make_async_remote_copy(
            sums1.at[slot], sums1.at[slot], p1_send.at[d], p1_recv.at[slot],
            device_id={"space": lax.rem(si + d, n_space)}, device_id_type=MESH)

    def copy2(d, slot):
        return pltpu.make_async_remote_copy(
            sums2.at[slot], sums2.at[slot], p2_send.at[d], p2_recv.at[slot],
            device_id={"tm": lax.rem(ti + d, n_tm)}, device_id_type=MESH)

    def copy3(d, slot):
        return pltpu.make_async_remote_copy(
            grads1.at[slot], grads1.at[slot], g1_send.at[d], g1_recv.at[slot],
            device_id={"space": lax.rem(si + d, n_space)}, device_id_type=MESH)

    def copy4(d, slot):
        return pltpu.make_async_remote_copy(
            grads2.at[slot], grads2.at[slot], g2_send.at[d], g2_recv.at[slot],
            device_id={"tm": lax.rem(ti + d, n_tm)}, device_id_type=MESH)

    def send_mode_gram():
        s_hi, s_lo = split(modes[...])
        two = dot(jnp.concatenate([s_hi, s_lo], axis=0), s_hi, NT)
        low = two[rows:]
        mode_gram = two[:rows] + (low + low.T)
        gram2[...] = jnp.concatenate([mode_gram, mode_gram], axis=1)
        sums1[si] = gram2[mine, :]
        for d in range(1, n_space):
            copy1(d, si).start()

    def send_newton():
        for d in range(1, n_space):
            copy1(d, lax.rem(si + d, n_space)).wait_recv()
        m2 = sums1[0]
        for s in range(1, n_space):
            m2 = m2 + sums1[s]
        both = jnp.concatenate([m2 * slope_gram[mine, :], m2 * slope_gram[below, :]], axis=0)
        u, v = iota((2 * rows, rows), 0), iota((2 * rows, rows), 1)
        take_cols = jnp.where(
            (lax.rem(u, rows) // 2 == v // 2) & (u // rows == lax.rem(v, 2)), 1.0, 0.0)
        u, v = iota((share, 2 * share), 0), iota((share, 2 * share), 1)
        take_rows = jnp.where(
            (lax.rem(v, share) // 2 == u // 2) & (v // share == lax.rem(u, 2)), 1.0, 0.0)
        newton = scale * dot(take_rows, dot(both, take_cols, NN, highest), NN, highest)
        sums2[ti] = jnp.concatenate([newton, jnp.zeros_like(newton)], axis=1)
        for d in range(1, n_tm):
            copy2(d, ti).start()

    ahead = min(AHEAD, chunks)
    gram_at = min(chunks - ahead + 1, chunks - 1)
    waited = 0
    for c in range(ahead):
        solve(c)
    for c in range(chunks):
        if c + ahead < chunks:
            solve(c + ahead)
        need = chunks if c >= gram_at else c + 1
        while waited < need:
            modes_copy(waited, 1 - core).wait_recv()
            waited += 1
        if c == gram_at:
            send_mode_gram()
        at = slice(c * CHUNK, (c + 1) * CHUNK)
        s_hi, s_lo = split(modes[:, at])
        fitted = dot(jnp.concatenate([s_hi, s_lo, s_hi], axis=0), b_three, TN)
        misfit = slab[at, :] - fitted
        slab[at, :] = misfit
        m_hi, m_lo = split(misfit)
        two = dot(jnp.concatenate([s_hi, s_lo], axis=0), m_hi, NN)
        moment = moment + ((two[rows:] + dot(s_hi, m_lo, NN)) + two[:rows])

    decay = jnp.sum(moment * slopes[:rows, here], axis=1, keepdims=True)
    turn = jnp.sum(moment * slopes[rows:, here], axis=1, keepdims=True)
    u, v = iota((rows, 2 * rows), 0), iota((rows, 2 * rows), 1)
    picked = jnp.where(lax.rem(v, 2) == 0, decay, turn)
    grads1[si] = jnp.sum(jnp.where(u // 2 == v // 2, picked, 0.0), axis=0, keepdims=True)
    for d in range(1, n_space):
        copy3(d, si).start()
    send_newton()
    for d in range(1, n_space):
        copy3(d, lax.rem(si + d, n_space)).wait_recv()
    grads2[ti] = jnp.sum(grads1[...], axis=0)
    for d in range(1, n_tm):
        copy4(d, ti).start()
    for d in range(1, n_tm):
        copy2(d, lax.rem(ti + d, n_tm)).wait_recv()
    for j in range(n_tm):
        newton_out[j * share:(j + 1) * share, :] = sums2[j, :, :rows]
    for d in range(1, n_tm):
        copy4(d, lax.rem(ti + d, n_tm)).wait_recv()
    grad_out[...] = jnp.sum(grads2[...], axis=0)[:, :rows] * -scale

    for c in range(chunks):
        core_copy(c).wait_send()
        for d in range(1, n_y):
            y_copy(c, d, yi).wait_send()
        modes_copy(c, core).wait_send()
    for d in range(1, n_space):
        copy1(d, si).wait_send()
        copy3(d, si).wait_send()
    for d in range(1, n_tm):
        copy2(d, ti).wait_send()
        copy4(d, ti).wait_send()


def local(n_space, n_tm, frame_slab, pair_decay_rates, pair_angular_frequencies):
    points, epochs = frame_slab.shape
    pairs = pair_decay_rates.shape[0]
    rows = 2 * pairs
    chunks = points // CHUNK
    n_y = n_tm // 2
    share = rows // n_tm
    hbm = pl.BlockSpec(memory_space=pltpu.HBM)
    vmem = pl.BlockSpec(memory_space=pltpu.VMEM)
    dma = pltpu.SemaphoreType.DMA
    shapes = (
        jax.ShapeDtypeStruct((rows, points), f32),
        jax.ShapeDtypeStruct((points, epochs), f32),
        jax.ShapeDtypeStruct((1, rows), f32),
        jax.ShapeDtypeStruct((rows, rows), f32),
    )
    operands = (frame_slab, pair_decay_rates[None, :], pair_angular_frequencies[None, :])
    modes, misfit, grad, newton = pl.pallas_call(
        functools.partial(kernel, n_space, n_tm, points * n_space),
        out_shape=shapes,
        in_specs=[hbm] * 3,
        out_specs=(vmem,) * 4,
        scratch_shapes=[
            pltpu.VMEM((1, pairs), f32),
            pltpu.VMEM((1, pairs), f32),
            pltpu.VMEM((rows, epochs * n_tm), f32),
            pltpu.VMEM((2 * rows, epochs * n_tm), f32),
            pltpu.VMEM((rows, points), f32),
            pltpu.VMEM((chunks, rows, HALF), f32),
            pltpu.VMEM((chunks, n_y, rows, HALF), f32),
            pltpu.VMEM((rows, 2 * rows), f32),
            pltpu.VMEM((2 * rows, 2 * rows), f32),
            pltpu.VMEM((n_space, share, 2 * rows), f32),
            pltpu.VMEM((n_tm, share, 2 * rows), f32),
            pltpu.VMEM((n_space, 1, 2 * rows), f32),
            pltpu.VMEM((n_tm, 1, 2 * rows), f32),
            dma((chunks,)), dma((2,)),
            dma((chunks,)), dma((chunks,)),
            dma((chunks, n_y)), dma((chunks, n_y)),
            dma((chunks,)), dma((chunks,)),
            dma((n_space,)), dma((n_space,)),
            dma((n_tm,)), dma((n_tm,)),
            dma((n_space,)), dma((n_space,)),
            dma((n_tm,)), dma((n_tm,)),
        ],
        compiler_params=pltpu.CompilerParams(
            collective_id=0, has_side_effects=True, vmem_limit_bytes=48 * 2**20
        ),
    )(*(pltpu.with_memory_space_constraint(x, pltpu.HBM) for x in operands))
    return modes, misfit, grad.reshape(rows), newton


def solution(mesh):
    return jax.shard_map(
        functools.partial(local, mesh.shape["space"], mesh.shape["tm"]),
        mesh=mesh,
        in_specs=(P("space", "tm"), P(), P()),
        out_specs=(P(None, "space"), P("space", "tm"), P(), P()),
        check_vma=False,
    )
```
